32 devices in a mesh: groups: 2 (over x), row: 4 (over y, core), col: 4 (over z).
Axes of the slice: x: 2, y: 2, z: 4, core: 2. Of those that a mesh axis runs over, the one named last changes fastest.
Arguments:
- zroot: float32 [4096, 2048], P(('groups', 'row')), parts along dimension 0, as said below
- panel_one: float32 [8, 2048, 1024], P(('groups', 'col'), 'row'), parts along dimension 0, may hold values from -0.125 to 0.125
- inv_one: float32 [8, 1024, 1024], P(('groups', 'col')), parts along dimension 0
- panel_two_j: float32 [16, 1024, 512], P(('groups', 'col'), 'row'), parts along dimension 0, may hold values from -0.109375 to 0.109375
- panel_two_r: float32 [16, 2048, 512], P(('groups', 'col'), 'row'), parts along dimension 0, may hold values from -0.109375 to 0.109375
- inv_two: float32 [16, 512, 512], P(('groups', 'col')), parts along dimension 0
- parents: int32 [16], P(('groups', 'col')), parts along dimension 0, may hold values from 0 to 3
- widths: int32 [16], P(('groups', 'col')), parts along dimension 0, may hold values from 256 to 512, as said below
- pattern_j: int32 [16, 16], P(('groups', 'col'), 'row'), parts along dimension 0, may hold values 0 or 1
- pattern_r: int32 [16, 32], P(('groups', 'col'), 'row'), parts along dimension 0, may hold values 0 or 1
Outputs:
- var_one: float32 [8, 1024], P(('groups', 'col'), 'row'), parts along dimension 0
- var_two: float32 [16, 512], P(('groups', 'col'), 'row'), parts along dimension 0
- z_two_j: float32 [16, 1024, 512], P(('groups', 'col'), 'row'), parts along dimension 0
- z_two_r: float32 [16, 2048, 512], P(('groups', 'col'), 'row'), parts along dimension 0
The draws below stay inside these ranges and needn't reach their ends.
There are 2 independent parts, one for each index of `groups`. The reference program is written for one: setup_inputs(seed, part) draws one part's arguments, and reference() takes and returns one part's arrays. A program takes and returns all parts, laid end to end along the dimension named above; each array names one. Nothing has to cross between parts.
Inputs may be any that keep to these rules, and one draw needn't show every extreme that they name: zroot is symmetric: it equals its transpose up to rounding, as a selected inverse block of a symmetric matrix does. `widths`: the live width of each level-2 supernode; columns at or past it are padding. `parents`: index of the level-1 parent of each level-2 supernode. `pattern_j`: 1 where a tile of 64 rows of the panel is stored. `pattern_r`: 1 where a tile of 64 rows of the panel is stored.
All inputs are finite; a program needn't handle non-finite values. No bound on the sum of `pattern_j` or of `pattern_r` on one device may be relied on, other than what follows from the above.
Results may differ from the reference program's by a relative error of at most 0.0003.
Values sent between devices are 32-bit elements; how exact they have to be, the bound alone decides.
No kernel may reach another device: no remote copies, remote signals or barrier semaphores. Data moves between devices by JAX's collectives and lax.ppermute only.
A program may use at most 128 MiB of HBM per device.

```python
import math
import jax
import jax.numpy as jnp
import numpy as np
from jax import lax

WR = 2048
W1 = 1024
W2 = 512
TILE = 64
P1 = 4
P2 = 8
WA = 3072


def triangle(key, count, width):
    first, second = jax.random.split(key)
    entries = jax.random.normal(first, (count, width, width), jnp.float32)
    diagonal = jax.random.uniform(second, (count, width), jnp.float32, 0.7, 1.4)
    lower = jnp.tril(entries, -1) * (0.5 / math.sqrt(width))
    return lower + diagonal[:, :, None] * jnp.eye(width, dtype=jnp.float32)


def draw_inv_one(key, part):
    return triangle(jax.random.fold_in(key, 11), P1, W1)


def draw_inv_two(key, part):
    return triangle(jax.random.fold_in(key, 23), P2, W2)


def draw_zroot(key, part):
    first, second = jax.random.split(jax.random.fold_in(key, 37), 2)
    noise = jax.random.normal(first, (WR, WR), jnp.float32)
    sym = (noise + noise.T) * (0.35 / math.sqrt(WR))
    diagonal = jax.random.uniform(second, (WR,), jnp.float32, 0.8, 1.6)
    base = sym + diagonal[:, None] * jnp.eye(WR, dtype=jnp.float32)
    return base


def draw_widths(key, part):
    first, second = jax.random.split(jax.random.fold_in(key, 41))
    values = jax.random.randint(first, (P2,), W2 // 2, W2 + 1)
    place = jax.random.randint(second, (), 0, P2)
    values = values.at[place].set(W2)
    values = values.at[(place + 1) % P2].set(W2 // 2)
    return values.astype(jnp.int32)


def touch_ends(values, key, least, high):
    spot = [jax.random.randint(jax.random.fold_in(key, axis), (), 0, length) for axis, length in enumerate(values.shape)]
    longest = values.shape.index(max(values.shape))
    beside = spot[:longest] + [(spot[longest] + 1) % values.shape[longest]] + spot[longest + 1:]
    return values.at[tuple(spot)].set(least).at[tuple(beside)].set(high)


def steps_of(rng, dims, cuts, low, high):
    factor_of, own = 1.0, jax.random.fold_in(rng, 6)
    for position, shards_of in cuts:
        heights = jnp.exp(jax.random.uniform(jax.random.fold_in(own, position), (shards_of,), jnp.float32, low / len(cuts), high / len(cuts)))
        factor_of = factor_of * jnp.repeat(heights, dims[position] // shards_of).reshape([-1 if axis == position else 1 for axis in range(len(dims))])
    return factor_of


def rank_bounds(number_of, skew):
    portions = [(1 << 20) // math.isqrt(grade ** skew) + 1 for grade in range(1, number_of + 1)]
    scale = 1 + sum(portions) // (1 << 30)
    return np.cumsum(np.array([max(1, weight // scale) for weight in portions]))


def ranked(own_key, shape, count, skew):
    grid = rank_bounds(count, skew)
    pick = jax.random.randint(jax.random.fold_in(own_key, 1), shape, 0, int(grid[count - 1]))
    grade = jnp.searchsorted(jnp.asarray(grid, jnp.int32), pick, side="right")
    return jax.random.permutation(jax.random.fold_in(own_key, 2), count)[grade].astype(jnp.int32)


def scatter_about(stream_key, dims, deviation, bound, cuts=(), kind=jnp.bfloat16):
    gain = steps_of(stream_key, dims, cuts, -0.22, 0.18) if cuts else 1.0
    values = jax.random.normal(stream_key, dims, jnp.float32) * deviation * gain
    return jnp.minimum(jnp.maximum(values, -bound), bound).astype(kind)


def setup_inputs(seed: int = 0, part: int = 0) -> dict:
    splits = jax.random.split(jax.random.key(seed), 11)
    part_splits = jax.random.split(jax.random.fold_in(splits[10], part), 11)
    zroot = draw_zroot(jax.random.fold_in(jax.random.fold_in(splits[10], part), 71), part)
    panel_one = scatter_about(part_splits[1], (P1, WR, W1), WR ** -0.5, 0.125, ((0, 4), (1, 4)), jnp.float32)
    inv_one = draw_inv_one(jax.random.fold_in(jax.random.fold_in(splits[10], part), 71), part)
    panel_two_j = scatter_about(part_splits[3], (P2, W1, W2), WA ** -0.5, 0.109375, ((0, 4), (1, 4)), jnp.float32)
    panel_two_r = scatter_about(part_splits[4], (P2, WR, W2), WA ** -0.5, 0.109375, ((0, 4), (1, 4)), jnp.float32)
    inv_two = draw_inv_two(jax.random.fold_in(jax.random.fold_in(splits[10], part), 71), part)
    parents = touch_ends(ranked(part_splits[6], (P2,), P1, 2), jax.random.fold_in(part_splits[6], 3), 0, P1 - 1).astype(jnp.int32)
    widths = draw_widths(jax.random.fold_in(jax.random.fold_in(splits[10], part), 71), part)
    pattern_j = touch_ends((jax.random.randint(part_splits[8], (P2, W1 // TILE), 0, 4) < 3).astype(jnp.int32), jax.random.fold_in(part_splits[8], 1), 0, 1)
    pattern_r = touch_ends((jax.random.randint(part_splits[9], (P2, WR // TILE), 0, 4) < 3).astype(jnp.int32), jax.random.fold_in(part_splits[9], 1), 0, 1)
    return dict(zroot=zroot, panel_one=panel_one, inv_one=inv_one, panel_two_j=panel_two_j, panel_two_r=panel_two_r, inv_two=inv_two, parents=parents, widths=widths, pattern_j=pattern_j, pattern_r=pattern_r)


def product(left, right):
    return jnp.dot(left, right, precision=lax.Precision.HIGHEST, preferred_element_type=jnp.float32)


def reference(zroot, panel_one, inv_one, panel_two_j, panel_two_r, inv_two, parents, widths, pattern_j, pattern_r):
    def level_one(pieces):
        panel, inverse = pieces
        factor = product(panel, inverse)
        root_block = -product(zroot, factor)
        diagonal_block = product(inverse.T, inverse) - product(factor.T, root_block)
        return root_block, diagonal_block

    all_rj, all_jj = lax.map(level_one, (panel_one, inv_one))
    var_one = jnp.diagonal(all_jj, axis1=1, axis2=2)

    def level_two(pieces):
        panel_j, panel_r, inverse, parent, width, tiles_j, tiles_r = pieces
        live = (jnp.arange(W2) < width).astype(jnp.float32)
        masked_j = panel_j * jnp.repeat(tiles_j.astype(jnp.float32), TILE)[:, None] * live[None, :]
        masked_r = panel_r * jnp.repeat(tiles_r.astype(jnp.float32), TILE)[:, None] * live[None, :]
        factor_j = product(masked_j, inverse)
        factor_r = product(masked_r, inverse)
        parent_jj = all_jj[parent]
        parent_rj = all_rj[parent]
        block_j = -(product(parent_jj, factor_j) + product(parent_rj.T, factor_r))
        block_r = -(product(parent_rj, factor_j) + product(zroot, factor_r))
        squares = jnp.sum(inverse * inverse, axis=0)
        variance = live * (squares - jnp.sum(factor_j * block_j, axis=0) - jnp.sum(factor_r * block_r, axis=0))
        return variance, block_j, block_r

    var_two, z_two_j, z_two_r = lax.map(level_two, (panel_two_j, panel_two_r, inv_two, parents, widths, pattern_j, pattern_r))
    return var_one, var_two, z_two_j, z_two_r
```

```python
import jax
import jax.numpy as jnp
from jax import lax
from jax.sharding import PartitionSpec as P

TILE = 64
CHUNKS = 4


def product(left, right):
    return jnp.dot(left, right, precision=lax.Precision.HIGH, preferred_element_type=jnp.float32)


def product_t(left, right):
    return lax.dot_general(
        left,
        right,
        (((0,), (0,)), ((), ())),
        precision=lax.Precision.HIGH,
        preferred_element_type=jnp.float32,
    )


def batched(form, left, right):
    return jnp.einsum(
        form, left, right, precision=lax.Precision.HIGH, preferred_element_type=jnp.float32
    )


def masked_factors(panel_two_j, panel_two_r, inv_two, live, pattern_j, pattern_r):
    mask_j = jnp.repeat(pattern_j.astype(jnp.float32), TILE, axis=1)
    mask_r = jnp.repeat(pattern_r.astype(jnp.float32), TILE, axis=1)
    masked_j = panel_two_j * mask_j[:, :, None] * live[:, None, :]
    masked_r = panel_two_r * mask_r[:, :, None] * live[:, None, :]
    return batched("nak,nkm->nam", masked_j, inv_two), batched("nak,nkm->nam", masked_r, inv_two)


def live_columns(widths, width_two):
    return (jnp.arange(width_two)[None, :] < widths[:, None]).astype(jnp.float32)


def general_body(
    zroot,
    panel_one,
    inv_one,
    panel_two_j,
    panel_two_r,
    inv_two,
    parents,
    widths,
    pattern_j,
    pattern_r,
):
    rows = lax.axis_size("row")
    row = lax.axis_index("row")
    inverse = inv_one[0]
    width_one = inverse.shape[0]
    share_one = width_one // rows
    nodes, width_two = inv_two.shape[0], inv_two.shape[1]
    factor = product(panel_one[0], inverse)
    own_columns = lax.dynamic_slice_in_dim(inverse, row * share_one, share_one, 1)
    square = product_t(own_columns, inverse)
    factors = lax.all_gather(factor, "col", axis=0)
    squares_of = lax.all_gather(square, "col", axis=0)
    whole = lax.all_gather(factor, "row", axis=0, tiled=True)
    terms = jnp.sum(factor * product(zroot, whole), axis=0)
    var_one = jnp.sum(own_columns * own_columns, axis=0) + lax.psum_scatter(
        terms, "row", scatter_dimension=0, tiled=True
    )
    live = live_columns(widths, width_two)
    factor_j, factor_r = masked_factors(
        panel_two_j, panel_two_r, inv_two, live, pattern_j, pattern_r
    )
    whole_j = lax.all_gather(factor_j, "row", axis=1, tiled=True)
    parent = jnp.take(factors, parents, axis=0)
    parent_square = jnp.take(squares_of, parents, axis=0)
    head = batched("nab,nbm->nam", parent, whole_j) - factor_r
    whole_head = lax.all_gather(head, "row", axis=1, tiled=True)
    block_r = batched("ab,nbm->nam", zroot, whole_head)
    own_j = batched("nab,nbm->nam", parent_square, whole_j)
    block_j = -(
        own_j
        + lax.psum_scatter(
            batched("nab,nam->nbm", parent, block_r), "row", scatter_dimension=1, tiled=True
        )
    )
    terms_two = jnp.sum(head * block_r, axis=1) + jnp.sum(factor_j * own_j, axis=1)
    summed = lax.psum_scatter(terms_two, "row", scatter_dimension=1, tiled=True)
    share_two = summed.shape[1]
    squares = jnp.sum(inv_two * inv_two, axis=1)
    live_share = lax.dynamic_slice_in_dim(live, row * share_two, share_two, 1)
    square_share = lax.dynamic_slice_in_dim(squares, row * share_two, share_two, 1)
    return var_one[None, :], live_share * (square_share + summed), block_j, block_r


ACROSS = [(0, 2), (2, 0), (1, 3), (3, 1)]
SIBLING = [(0, 1), (1, 0), (2, 3), (3, 2)]
INNER = [(1, 2), (2, 1)]
INWARD = [(0, 1), (3, 2)]
OUTWARD = [(1, 0), (2, 3)]


def line_body(
    zroot,
    panel_one,
    inv_one,
    panel_two_j,
    panel_two_r,
    inv_two,
    parents,
    widths,
    pattern_j,
    pattern_r,
):
    rows, cols = 4, 4
    row = lax.axis_index("row")
    col = lax.axis_index("col")
    chip, core = row // 2, row % 2
    root_rows = zroot.shape[0]
    inverse = inv_one[0]
    width_one = inverse.shape[0]
    share_one = width_one // rows
    nodes, width_two = inv_two.shape[0], inv_two.shape[1]
    part = root_rows // CHUNKS

    mirror = col >= cols // 2
    place = jnp.where(mirror, cols - 1 - col, col)

    def seen(index):
        return jnp.where(mirror, cols - 1 - index, index)

    outer_needs = seen(lax.ppermute(parents, "col", INWARD))
    outer_one = jnp.any(outer_needs == 1)
    outer_three = jnp.any(outer_needs == 3)
    needs = seen(parents)
    need_one = jnp.any(needs == 1)

    own = [product(panel_one[0, q * part : (q + 1) * part], inverse) for q in range(CHUNKS)]
    own_columns = lax.dynamic_slice_in_dim(inverse, row * share_one, share_one, 1)
    square = product_t(own_columns, inverse)
    pieces = own + [square[:part], square[part:]]

    def relay(piece):
        inner = lax.ppermute(piece, "col", INNER)
        outer = lax.ppermute(piece, "col", INWARD)
        far = lax.ppermute(outer, "col", INNER)
        first = lax.ppermute(jnp.where(outer_one, piece, inner), "col", OUTWARD)
        second = lax.ppermute(jnp.where(outer_three, far, inner), "col", OUTWARD)
        chosen = []
        for n in range(nodes):
            p = needs[n]
            at_end = jnp.where(
                (p == 3) | ((p == 2) & need_one), second, jnp.where(p == 0, piece, first)
            )
            inside = jnp.where(
                p == 0, outer, jnp.where(p == 1, piece, jnp.where(p == 2, inner, far))
            )
            chosen.append(jnp.where(place == 0, at_end, inside))
        return chosen

    live = live_columns(widths, width_two)
    factor_j, factor_r = masked_factors(
        panel_two_j, panel_two_r, inv_two, live, pattern_j, pattern_r
    )
    whole_j = lax.all_gather(factor_j, "row", axis=1, tiled=True)

    factor = jnp.concatenate(own, axis=0)
    half = width_one // 2

    def halves(x, which):
        return lax.dynamic_slice_in_dim(x, which * half, half, 1)

    def root_columns(which):
        return lax.dynamic_slice_in_dim(zroot, which * root_rows, root_rows, 1)

    across_same = lax.ppermute(halves(factor, 1 - chip), "row", ACROSS)
    across_other = lax.ppermute(across_same, "row", SIBLING)
    sibling = lax.ppermute(halves(factor, 1 - core), "row", SIBLING)
    terms = jnp.sum(factor * product(root_columns(row), factor), axis=0)
    beside = 2 * jnp.sum(
        halves(factor, core) * product(root_columns(2 * chip + 1 - core), sibling), axis=0
    )
    beyond = 2 * jnp.sum(
        halves(factor, chip)
        * (
            product(root_columns(2 * (1 - chip) + core), across_same)
            + product(root_columns(2 * (1 - chip) + 1 - core), across_other)
        ),
        axis=0,
    )
    first_half = (jnp.arange(width_one) < half).astype(jnp.float32)

    def spread(x, which):
        return jnp.concatenate([x, x]) * jnp.where(which == 0, first_half, 1 - first_half)

    terms_one = terms + spread(beside, core) + spread(beyond, chip)

    root_parts = zroot.reshape(root_rows, rows, CHUNKS, part).transpose(2, 0, 1, 3)
    taken, heads = [], []
    block_r = None
    for q in range(CHUNKS):
        chosen = relay(pieces[q])
        taken.append(chosen)
        head = jnp.concatenate(
            [
                product(chosen[n], whole_j[n]) - factor_r[n, q * part : (q + 1) * part]
                for n in range(nodes)
            ],
            axis=1,
        )
        heads.append(head)
        whole_head = lax.all_gather(head, "row", axis=0, tiled=True)
        term = product(root_parts[q].reshape(root_rows, rows * part), whole_head)
        block_r = term if block_r is None else block_r + term
    square_parts = [relay(piece) for piece in pieces[CHUNKS:]]

    blocks_j, terms_two = [], []
    for n in range(nodes):
        columns = slice(n * width_two, (n + 1) * width_two)
        z = block_r[:, columns]
        parent = jnp.concatenate([t[n] for t in taken], axis=0)
        parent = parent.reshape(root_rows, 2, 2, share_one)

        def towards(which):
            block = lax.dynamic_index_in_dim(parent, which, 2, keepdims=False)
            return product_t(block.reshape(root_rows, 2 * share_one), z)

        summed = towards(core) + lax.ppermute(towards(1 - core), "row", SIBLING)
        summed = summed.reshape(2, share_one, width_two)
        mine = lax.dynamic_index_in_dim(summed, chip, 0, keepdims=False)
        theirs = lax.dynamic_index_in_dim(summed, 1 - chip, 0, keepdims=False)
        own_j = product(jnp.concatenate([t[n] for t in square_parts], axis=0), whole_j[n])
        blocks_j.append(-(own_j + mine + lax.ppermute(theirs, "row", ACROSS)))
        head = jnp.concatenate([h[:, columns] for h in heads], axis=0)
        terms_two.append(jnp.sum(head * z, axis=0) + jnp.sum(factor_j[n] * own_j, axis=0))
    block_j = jnp.stack(blocks_j)
    z_two_r = jnp.stack([block_r[:, n * width_two : (n + 1) * width_two] for n in range(nodes)])

    share_two = width_two // rows
    packed = jnp.concatenate(
        [terms_one.reshape(rows, share_one)] + [t.reshape(rows, share_two) for t in terms_two],
        axis=1,
    ).reshape(2, 2, -1)
    packed = lax.dynamic_index_in_dim(packed, core, 1, keepdims=False) + lax.ppermute(
        lax.dynamic_index_in_dim(packed, 1 - core, 1, keepdims=False), "row", SIBLING
    )
    packed = lax.dynamic_index_in_dim(packed, chip, 0, keepdims=False) + lax.ppermute(
        lax.dynamic_index_in_dim(packed, 1 - chip, 0, keepdims=False), "row", ACROSS
    )
    var_one = packed[:share_one] + jnp.sum(own_columns * own_columns, axis=0)
    squares = jnp.sum(inv_two * inv_two, axis=1)
    live_share = lax.dynamic_slice_in_dim(live, row * share_two, share_two, 1)
    square_share = lax.dynamic_slice_in_dim(squares, row * share_two, share_two, 1)
    var_two = live_share * (square_share + packed[share_one:].reshape(nodes, share_two))
    return var_one[None, :], var_two, block_j, z_two_r


def solution(mesh):
    line = mesh.shape["row"] == 4 and mesh.shape["col"] == 4

    def body(*args):
        two_nodes = args[5].shape[0] == 2
        return (line_body if line and two_nodes else general_body)(*args)

    return jax.shard_map(
        body,
        mesh=mesh,
        in_specs=(
            P(("groups", "row"), None),
            P(("groups", "col"), "row", None),
            P(("groups", "col"), None, None),
            P(("groups", "col"), "row", None),
            P(("groups", "col"), "row", None),
            P(("groups", "col"), None, None),
            P(("groups", "col")),
            P(("groups", "col")),
            P(("groups", "col"), "row"),
            P(("groups", "col"), "row"),
        ),
        out_specs=(
            P(("groups", "col"), "row"),
            P(("groups", "col"), "row"),
            P(("groups", "col"), "row", None),
            P(("groups", "col"), "row", None),
        ),
        check_vma=False,
    )
```

```python
import jax
import jax.numpy as jnp
from jax import lax
from jax.experimental import pallas as pl
from jax.experimental.pallas import tpu as pltpu
from jax.sharding import PartitionSpec as P

TILE = 64
CHUNKS = 4


def product(left, right):
    return jnp.dot(left, right, precision=lax.Precision.HIGH, preferred_element_type=jnp.float32)


def product_t(left, right):
    return lax.dot_general(
        left,
        right,
        (((0,), (0,)), ((), ())),
        precision=lax.Precision.HIGH,
        preferred_element_type=jnp.float32,
    )


def batched(form, left, right):
    return jnp.einsum(
        form, left, right, precision=lax.Precision.HIGH, preferred_element_type=jnp.float32
    )


def masked_factors(panel_two_j, panel_two_r, inv_two, live, pattern_j, pattern_r):
    mask_j = jnp.repeat(pattern_j.astype(jnp.float32), TILE, axis=1)
    mask_r = jnp.repeat(pattern_r.astype(jnp.float32), TILE, axis=1)
    masked_j = panel_two_j * mask_j[:, :, None] * live[:, None, :]
    masked_r = panel_two_r * mask_r[:, :, None] * live[:, None, :]
    return batched("nak,nkm->nam", masked_j, inv_two), batched("nak,nkm->nam", masked_r, inv_two)


def live_columns(widths, width_two):
    return (jnp.arange(width_two)[None, :] < widths[:, None]).astype(jnp.float32)


def general_body(
    zroot,
    panel_one,
    inv_one,
    panel_two_j,
    panel_two_r,
    inv_two,
    parents,
    widths,
    pattern_j,
    pattern_r,
):
    rows = lax.axis_size("row")
    row = lax.axis_index("row")
    inverse = inv_one[0]
    width_one = inverse.shape[0]
    share_one = width_one // rows
    nodes, width_two = inv_two.shape[0], inv_two.shape[1]
    factor = product(panel_one[0], inverse)
    own_columns = lax.dynamic_slice_in_dim(inverse, row * share_one, share_one, 1)
    square = product_t(own_columns, inverse)
    factors = lax.all_gather(factor, "col", axis=0)
    squares_of = lax.all_gather(square, "col", axis=0)
    whole = lax.all_gather(factor, "row", axis=0, tiled=True)
    terms = jnp.sum(factor * product(zroot, whole), axis=0)
    var_one = jnp.sum(own_columns * own_columns, axis=0) + lax.psum_scatter(
        terms, "row", scatter_dimension=0, tiled=True
    )
    live = live_columns(widths, width_two)
    factor_j, factor_r = masked_factors(
        panel_two_j, panel_two_r, inv_two, live, pattern_j, pattern_r
    )
    whole_j = lax.all_gather(factor_j, "row", axis=1, tiled=True)
    parent = jnp.take(factors, parents, axis=0)
    parent_square = jnp.take(squares_of, parents, axis=0)
    head = batched("nab,nbm->nam", parent, whole_j) - factor_r
    whole_head = lax.all_gather(head, "row", axis=1, tiled=True)
    block_r = batched("ab,nbm->nam", zroot, whole_head)
    own_j = batched("nab,nbm->nam", parent_square, whole_j)
    block_j = -(
        own_j
        + lax.psum_scatter(
            batched("nab,nam->nbm", parent, block_r), "row", scatter_dimension=1, tiled=True
        )
    )
    terms_two = jnp.sum(head * block_r, axis=1) + jnp.sum(factor_j * own_j, axis=1)
    summed = lax.psum_scatter(terms_two, "row", scatter_dimension=1, tiled=True)
    share_two = summed.shape[1]
    squares = jnp.sum(inv_two * inv_two, axis=1)
    live_share = lax.dynamic_slice_in_dim(live, row * share_two, share_two, 1)
    square_share = lax.dynamic_slice_in_dim(squares, row * share_two, share_two, 1)
    return var_one[None, :], live_share * (square_share + summed), block_j, block_r


ACROSS = [(0, 2), (2, 0), (1, 3), (3, 1)]
SIBLING = [(0, 1), (1, 0), (2, 3), (3, 2)]
INNER = [(1, 2), (2, 1)]
INWARD = [(0, 1), (3, 2)]
OUTWARD = [(1, 0), (2, 3)]


VMEM_LIMIT = 48 * 1024 * 1024
ANYWHERE = pl.BlockSpec(memory_space=pl.ANY)
SCALARS = pl.BlockSpec(memory_space=pltpu.SMEM)
WHOLE = pl.BlockSpec(memory_space=pltpu.VMEM)


def cost():
    return pl.CostEstimate(flops=1, bytes_accessed=1, transcendentals=0)


def params(**more):
    return pltpu.CompilerParams(vmem_limit_bytes=VMEM_LIMIT, **more)


def split(x):
    high = x.astype(jnp.bfloat16)
    return high, (x - high.astype(jnp.float32)).astype(jnp.bfloat16)


def three(left, right, contract=((1,), (0,))):
    def dot(a, b):
        return lax.dot_general(a, b, (contract, ((), ())), preferred_element_type=jnp.float32)

    return dot(left[0], right[0]) + (dot(left[0], right[1]) + dot(left[1], right[0]))


def level_one(panel, inverse, sizes):
    root_rows, width = panel.shape
    tile = 256
    starts = [sum(sizes[:q]) for q in range(len(sizes))]

    def kernel(panel_ref, inverse_ref, *refs):
        outs, (high, low) = refs[: len(sizes)], refs[len(sizes) :]

        @pl.when(pl.program_id(0) == 0)
        def _():
            high[...], low[...] = split(panel_ref[...])

        result = three((high[...], low[...]), split(inverse_ref[...]))
        for q, size in enumerate(sizes):
            outs[q][...] = result[starts[q] : starts[q] + size]

    return pl.pallas_call(
        kernel,
        grid=(width // tile,),
        in_specs=[
            pl.BlockSpec((root_rows, width), lambda i: (0, 0)),
            pl.BlockSpec((width, tile), lambda i: (0, i)),
        ],
        out_specs=[pl.BlockSpec((size, tile), lambda i: (0, i)) for size in sizes],
        out_shape=[jax.ShapeDtypeStruct((size, width), jnp.float32) for size in sizes],
        scratch_shapes=[pltpu.VMEM((root_rows, width), jnp.bfloat16)] * 2,
        compiler_params=params(),
        cost_estimate=cost(),
    )(panel, inverse)


def route(flags, picks, releases, deps):
    count = len(picks)
    used = 2 * count + len(releases)

    def kernel(flags_ref, *refs):
        outs = refs[used + len(deps) :]
        for k, (which, _, _) in enumerate(picks):

            @pl.when(flags_ref[which] == 1)
            def _():
                outs[k][...] = refs[2 * k][...]

            @pl.when(flags_ref[which] != 1)
            def _():
                outs[k][...] = refs[2 * k + 1][...]

        for k in range(len(releases)):
            outs[count + k][...] = refs[2 * count + k][...]

    operands = [x for _, yes, no in picks for x in (yes, no)] + releases
    results = [yes for _, yes, _ in picks] + releases
    return pl.pallas_call(
        kernel,
        in_specs=[SCALARS] + [WHOLE] * used + [ANYWHERE] * len(deps),
        out_specs=[WHOLE] * len(results),
        out_shape=[jax.ShapeDtypeStruct(x.shape, x.dtype) for x in results],
        compiler_params=params(),
        cost_estimate=cost(),
    )(flags, *operands, *deps)


def square_parts(columns, inverse, part, deps):
    depth, share = columns.shape
    width = inverse.shape[1]
    tile = 256
    count = share // part

    def kernel(columns_ref, inverse_ref, *refs):
        outs, (high, low) = refs[len(deps) : len(deps) + count], refs[len(deps) + count :]

        @pl.when(pl.program_id(0) == 0)
        def _():
            high[...], low[...] = split(columns_ref[...])

        result = three((high[...], low[...]), split(inverse_ref[...]), ((0,), (0,)))
        for q in range(count):
            outs[q][...] = result[q * part : (q + 1) * part]

    return pl.pallas_call(
        kernel,
        grid=(width // tile,),
        in_specs=[
            pl.BlockSpec((depth, share), lambda i: (0, 0)),
            pl.BlockSpec((depth, tile), lambda i: (0, i)),
        ]
        + [ANYWHERE] * len(deps),
        out_specs=[pl.BlockSpec((part, tile), lambda i: (0, i))] * count,
        out_shape=[jax.ShapeDtypeStruct((part, width), jnp.float32)] * count,
        scratch_shapes=[pltpu.VMEM((depth, share), jnp.bfloat16)] * 2,
        compiler_params=params(),
        cost_estimate=cost(),
    )(columns, inverse, *deps)


def with_parent(choice, candidates, whole_j, minus, start, deps):
    nodes, depth, width = whole_j.shape
    listed = isinstance(candidates, list)
    part = candidates[0].shape[0]
    sources_in = candidates if listed else [candidates]
    count = len(sources_in)
    extra = [] if minus is None else [minus]

    def kernel(choice_ref, *refs):
        sources = refs[:count]
        whole_ref = refs[count]
        minus_ref = refs[count + 1] if extra else None
        out_ref, chosen_ref, sems = refs[-3:]
        for n in range(nodes):
            if not listed:
                source = sources[0].at[choice_ref[n]]
                pltpu.make_async_copy(source, chosen_ref.at[n], sems.at[n]).start()
                continue
            for k in range(count):

                @pl.when(choice_ref[n] == k)
                def _():
                    pltpu.make_async_copy(sources[k], chosen_ref.at[n], sems.at[n]).start()

        for n in range(nodes):
            source = sources[0] if listed else sources[0].at[0]
            pltpu.make_async_copy(source, chosen_ref.at[n], sems.at[n]).wait()
            result = three(split(chosen_ref[n]), split(whole_ref[n]))
            if extra:
                result = result - minus_ref[n]
            out_ref[:, n * width : (n + 1) * width] = result

    return pl.pallas_call(
        kernel,
        grid=(1,),
        in_specs=[SCALARS]
        + [ANYWHERE] * count
        + [pl.BlockSpec((nodes, depth, width), lambda i: (0, 0, 0))]
        + [pl.BlockSpec((nodes, part, width), lambda i: (0, start // part, 0))] * len(extra)
        + [ANYWHERE] * len(deps),
        out_specs=[
            pl.BlockSpec((part, nodes * width), lambda i: (0, 0)),
            pl.BlockSpec((nodes, part, depth), lambda i: (0, 0, 0)),
        ],
        out_shape=[
            jax.ShapeDtypeStruct((part, nodes * width), jnp.float32),
            jax.ShapeDtypeStruct((nodes, part, depth), jnp.float32),
        ],
        scratch_shapes=[pltpu.SemaphoreType.DMA((nodes,))],
        compiler_params=params(),
        cost_estimate=cost(),
    )(choice, *sources_in, whole_j, *extra, *deps)


def in_order(order, blocks, deps):
    nodes, share, width = blocks[0].shape
    count = len(blocks)

    def kernel(order_ref, *refs):
        out_ref = refs[-1]
        for k in range(count):
            start = pl.multiple_of(order_ref[k] * share, share)
            for n in range(nodes):
                out_ref[n, pl.ds(start, share), :] = refs[k][n]

    return pl.pallas_call(
        kernel,
        in_specs=[SCALARS] + [WHOLE] * count + [ANYWHERE] * len(deps),
        out_specs=WHOLE,
        out_shape=jax.ShapeDtypeStruct((nodes, count * share, width), jnp.float32),
        compiler_params=params(),
        cost_estimate=cost(),
    )(order, *blocks, *deps)


def halves_of(place, own, deps):
    width = own[0].shape[1]
    half = width // 2
    starts = [sum(x.shape[0] for x in own[:q]) for q in range(len(own))]
    rows = sum(x.shape[0] for x in own)

    def kernel(place_ref, *refs):
        outs = refs[len(own) + len(deps) :]
        for k in range(2):
            at = pl.ds(pl.multiple_of((1 - place_ref[k]) * half, half), half)
            for q, x in enumerate(own):
                outs[k][starts[q] : starts[q] + x.shape[0], :] = refs[q][:, at]

    return pl.pallas_call(
        kernel,
        in_specs=[SCALARS] + [WHOLE] * len(own) + [ANYWHERE] * len(deps),
        out_specs=[WHOLE] * 2,
        out_shape=[jax.ShapeDtypeStruct((rows, half), jnp.float32)] * 2,
        compiler_params=params(),
        cost_estimate=cost(),
    )(place, *own, *deps)


def pair_terms(heads, block_r, deps):
    nodes, _, width = block_r.shape
    starts = [sum(x.shape[0] for x in heads[:q]) for q in range(len(heads))]

    def kernel(*refs):
        block_ref, out_ref = refs[len(heads)], refs[-1]
        for n in range(nodes):
            total = jnp.zeros((1, width), jnp.float32)
            for q, head in enumerate(heads):
                total = total + jnp.sum(
                    refs[q][:, n * width : (n + 1) * width]
                    * block_ref[n, starts[q] : starts[q] + head.shape[0], :],
                    axis=0,
                    keepdims=True,
                )
            out_ref[n : n + 1, :] = total

    return pl.pallas_call(
        kernel,
        in_specs=[WHOLE] * (len(heads) + 1) + [ANYWHERE] * len(deps),
        out_specs=WHOLE,
        out_shape=jax.ShapeDtypeStruct((nodes, width), jnp.float32),
        compiler_params=params(),
        cost_estimate=cost(),
    )(*heads, block_r, *deps)


def root_terms(place, zroot, own, sibling, across_same, across_other, deps):
    root_rows = zroot.shape[0]
    width = own[0].shape[1]
    half = width // 2
    count = len(own)
    starts = [sum(x.shape[0] for x in own[:q]) for q in range(count)]

    def kernel(place_ref, root_ref, *refs):
        sibling_ref, same_ref, other_ref = refs[count : count + 3]
        out_ref, factor = refs[-2:]
        chip, core = place_ref[0], place_ref[1]
        for q, x in enumerate(own):
            factor[starts[q] : starts[q] + x.shape[0], :] = refs[q][...]

        def root(which):
            start = pl.multiple_of(which * root_rows, root_rows)
            return split(root_ref[:, pl.ds(start, root_rows)])

        def halved(which):
            return factor[:, pl.ds(pl.multiple_of(which * half, half), half)]

        def put(which, value):
            at = pl.ds(pl.multiple_of(which * half, half), half)
            out_ref[:, at] = out_ref[:, at] + 2 * jnp.sum(value, axis=0, keepdims=True)

        out_ref[...] = jnp.sum(
            factor[...] * three(root(2 * chip + core), split(factor[...])), axis=0, keepdims=True
        )
        put(core, halved(core) * three(root(2 * chip + 1 - core), split(sibling_ref[...])))
        put(
            chip,
            halved(chip)
            * (
                three(root(2 * (1 - chip) + core), split(same_ref[...]))
                + three(root(2 * (1 - chip) + 1 - core), split(other_ref[...]))
            ),
        )

    return pl.pallas_call(
        kernel,
        in_specs=[SCALARS] + [WHOLE] * (1 + count + 3) + [ANYWHERE] * len(deps),
        out_specs=WHOLE,
        out_shape=jax.ShapeDtypeStruct((1, width), jnp.float32),
        scratch_shapes=[pltpu.VMEM((root_rows, width), jnp.float32)],
        compiler_params=params(),
        cost_estimate=cost(),
    )(place, zroot, *own, sibling, across_same, across_other, *deps)


def root_step(order, zroot, start, parts, before, nodes, deps):
    root_rows = zroot.shape[0]
    size, columns = parts[0].shape
    width = columns // nodes
    count = len(parts)
    tile = 256
    tiles = width // tile
    extra = [] if before is None else [before]

    def kernel(order_ref, *refs):
        out_ref, high, low, head_high, head_low = refs[-5:]
        heads = refs[count : 2 * count]

        @pl.when(pl.program_id(0) == 0)
        def _():
            for k in range(count):
                at = slice(k * size, (k + 1) * size)
                high[:, at], low[:, at] = split(refs[k][...])

        for k in range(count):
            at = slice(k * size, (k + 1) * size)
            head_high[at, :], head_low[at, :] = split(heads[k][...])
        result = three((high[...], low[...]), (head_high[...], head_low[...]))
        out_ref[...] = result + refs[2 * count][...] if extra else result

    def root_block(k):
        return pl.BlockSpec(
            (root_rows, size), lambda i, order: (0, order[k] * (root_rows // size) + start // size)
        )

    block = pl.BlockSpec((None, root_rows, tile), lambda i, order: (i // tiles, 0, i % tiles))
    return pl.pallas_call(
        kernel,
        grid_spec=pltpu.PrefetchScalarGridSpec(
            num_scalar_prefetch=1,
            grid=(nodes * tiles,),
            in_specs=[root_block(k) for k in range(count)]
            + [pl.BlockSpec((size, tile), lambda i, order: (0, i))] * count
            + [block] * len(extra)
            + [ANYWHERE] * len(deps),
            out_specs=block,
            scratch_shapes=[pltpu.VMEM((root_rows, count * size), jnp.bfloat16)] * 2
            + [pltpu.VMEM((count * size, tile), jnp.bfloat16)] * 2,
        ),
        out_shape=jax.ShapeDtypeStruct((nodes, root_rows, width), jnp.float32),
        compiler_params=params(),
        cost_estimate=cost(),
    )(order, *[zroot] * count, *parts, *extra, *deps)


def transposed(which, taken, node, block_r, deps):
    depth = taken[0].shape[2]
    _, rows, width = block_r.shape
    share = depth // 4
    count = len(taken)
    starts = [sum(x.shape[1] for x in taken[:q]) for q in range(count)]

    def kernel(which_ref, *refs):
        block_ref = refs[count]
        out_ref, left = refs[-2:]
        for q, x in enumerate(taken):
            for chip in range(2):
                start = pl.multiple_of((2 * chip + which_ref[0]) * share, share)
                left[
                    starts[q] : starts[q] + x.shape[1], chip * share : (chip + 1) * share
                ] = refs[q][:, pl.ds(start, share)]
        out_ref[...] = three(split(left[...]), split(block_ref[...]), ((0,), (0,)))

    return pl.pallas_call(
        kernel,
        grid=(1,),
        in_specs=[SCALARS]
        + [pl.BlockSpec((None,) + x.shape[1:], lambda i: (node, 0, 0)) for x in taken]
        + [pl.BlockSpec((None, rows, width), lambda i: (node, 0, 0))]
        + [ANYWHERE] * len(deps),
        out_specs=pl.BlockSpec((2 * share, width), lambda i: (0, 0)),
        out_shape=jax.ShapeDtypeStruct((2 * share, width), jnp.float32),
        scratch_shapes=[pltpu.VMEM((rows, 2 * share), jnp.float32)],
        compiler_params=params(),
        cost_estimate=cost(),
    )(which, *taken, block_r, *deps)


def line_body(
    zroot,
    panel_one,
    inv_one,
    panel_two_j,
    panel_two_r,
    inv_two,
    parents,
    widths,
    pattern_j,
    pattern_r,
):
    rows, cols = 4, 4
    row = lax.axis_index("row")
    col = lax.axis_index("col")
    chip, core = row // 2, row % 2
    root_rows = zroot.shape[0]
    inverse = inv_one[0]
    width_one = inverse.shape[0]
    share_one = width_one // rows
    nodes, width_two = inv_two.shape[0], inv_two.shape[1]

    mirror = col >= cols // 2
    at_end = jnp.where(mirror, cols - 1 - col, col) == 0

    def seen(index):
        return jnp.where(mirror, cols - 1 - index, index)

    outer_parents = lax.ppermute(parents, "col", INWARD)
    outer_needs = seen(outer_parents)
    flags = jnp.stack([jnp.any(outer_needs == 1), jnp.any(outer_needs == 3)]).astype(jnp.int32)
    needs = seen(parents)
    end_choice = jnp.where(
        (needs == 3) | ((needs == 2) & jnp.any(needs == 1)), 5, jnp.where(needs == 0, 0, 4)
    )
    inside_choice = jnp.where(
        needs == 0, 1, jnp.where(needs == 1, 0, jnp.where(needs == 2, 2, 3))
    )
    choice = jnp.where(at_end, end_choice, inside_choice).astype(jnp.int32)
    here = jnp.stack([chip, core]).astype(jnp.int32)

    order = jnp.stack([row, row ^ 1, row ^ 2, row ^ 3]).astype(jnp.int32)
    chain = []

    def exchange(x):
        across = lax.ppermute(x, "row", ACROSS)
        beside = lax.ppermute(x, "row", SIBLING)
        return [x, beside, across, lax.ppermute(across, "row", SIBLING)]

    sizes = [root_rows // CHUNKS] * CHUNKS
    starts = [sum(sizes[:q]) for q in range(CHUNKS)]
    own = list(level_one(panel_one[0], inverse, sizes))
    gathered = [lax.all_gather(x, "col", axis=0) for x in own]
    own_columns = lax.dynamic_slice_in_dim(inverse, row * share_one, share_one, 1)
    (square,) = square_parts(own_columns, inverse, share_one, [own[0], outer_parents])
    chain.append([square])

    live = live_columns(widths, width_two)
    factor_j, factor_r = masked_factors(
        panel_two_j, panel_two_r, inv_two, live, pattern_j, pattern_r
    )
    shares_j = exchange(factor_j)
    whole_j = in_order(order, shares_j, chain[-1])
    chain.append([whole_j])
    to_chip, to_core = halves_of(here, own, chain[-1])
    chain.append([to_chip])
    across_same = lax.ppermute(to_chip, "row", ACROSS)
    across_other = lax.ppermute(across_same, "row", SIBLING)
    sibling = lax.ppermute(to_core, "row", SIBLING)

    heads, taken, wholes = [], [], []
    parents_here = parents.astype(jnp.int32)

    def parent_step(q, also=()):
        deps = list(chain[-1]) + list(also)
        out, chosen = with_parent(parents_here, gathered[q], whole_j, factor_r, starts[q], deps)
        heads.append(out)
        taken.append(chosen)
        wholes.append(exchange(out))
        chain.append([out])

    def gather_step(q, before):
        out = root_step(order, zroot, starts[q], wholes[q], before, nodes, chain[-1])
        chain.append([out])
        return out

    def route_step(*picks, also=()):
        moved = list(route(flags, list(picks), [], list(chain[-1]) + list(also)))
        chain.append([moved[0]])
        return [lax.ppermute(x, "col", OUTWARD) for x in moved]

    parent_step(0)
    terms_one = root_terms(here, zroot, own, sibling, across_same, across_other, chain[-1])
    chain.append([terms_one])
    parent_step(1, wholes[0])
    block_r = gather_step(0, None)
    parent_step(2, wholes[1])
    (released,) = route(flags, [], [square], chain[-1])
    inner = lax.ppermute(released, "col", INNER)
    outer = lax.ppermute(released, "col", INWARD)
    block_r = gather_step(1, block_r)
    parent_step(3, wholes[2])
    far = lax.ppermute(outer, "col", INNER)
    (first,) = route_step((0, square, inner), also=[outer])
    block_r = gather_step(2, block_r)
    block_r = gather_step(3, block_r)
    received, kept, sums = [], [], []
    for n in range(nodes):
        which = (1 - core)[None].astype(jnp.int32)
        sent = transposed(which, taken, n, block_r, chain[-1])
        received.append(lax.ppermute(sent, "row", SIBLING))
        chain.append([sent])
    (second,) = route_step((1, far, inner))
    for n in range(nodes):
        which = core[None].astype(jnp.int32)
        keep = transposed(which, taken, n, block_r, chain[-1])
        kept.append(keep)
        chain.append([keep])
    for n in range(nodes):
        both = (kept[n] + received[n]).reshape(2, share_one, width_two)
        mine = lax.dynamic_index_in_dim(both, chip, 0, keepdims=False)
        theirs = lax.dynamic_index_in_dim(both, 1 - chip, 0, keepdims=False)
        sums.append(mine + lax.ppermute(theirs, "row", ACROSS))
    pairs = pair_terms(heads, block_r, chain[-1])
    chain.append([pairs])
    own_rows, _ = with_parent(
        choice, [square, outer, inner, far, first, second], whole_j, None, 0, chain[-1]
    )
    blocks_j, terms_two = [], []
    for n in range(nodes):
        own_j = own_rows[:, n * width_two : (n + 1) * width_two]
        blocks_j.append(-(own_j + sums[n]))
        terms_two.append(pairs[n] + jnp.sum(factor_j[n] * own_j, axis=0))
    block_j = jnp.stack(blocks_j)

    share_two = width_two // rows
    packed = jnp.concatenate(
        [terms_one.reshape(rows, share_one)] + [t.reshape(rows, share_two) for t in terms_two],
        axis=1,
    ).reshape(2, 2, -1)
    packed = lax.dynamic_index_in_dim(packed, core, 1, keepdims=False) + lax.ppermute(
        lax.dynamic_index_in_dim(packed, 1 - core, 1, keepdims=False), "row", SIBLING
    )
    packed = lax.dynamic_index_in_dim(packed, chip, 0, keepdims=False) + lax.ppermute(
        lax.dynamic_index_in_dim(packed, 1 - chip, 0, keepdims=False), "row", ACROSS
    )
    var_one = packed[:share_one] + jnp.sum(own_columns * own_columns, axis=0)
    squares = jnp.sum(inv_two * inv_two, axis=1)
    live_share = lax.dynamic_slice_in_dim(live, row * share_two, share_two, 1)
    square_share = lax.dynamic_slice_in_dim(squares, row * share_two, share_two, 1)
    var_two = live_share * (square_share + packed[share_one:].reshape(nodes, share_two))
    return var_one[None, :], var_two, block_j, block_r


def solution(mesh):
    line = mesh.shape["row"] == 4 and mesh.shape["col"] == 4

    def body(*args):
        two_nodes = args[5].shape[0] == 2
        return (line_body if line and two_nodes else general_body)(*args)

    return jax.shard_map(
        body,
        mesh=mesh,
        in_specs=(
            P(("groups", "row"), None),
            P(("groups", "col"), "row", None),
            P(("groups", "col"), None, None),
            P(("groups", "col"), "row", None),
            P(("groups", "col"), "row", None),
            P(("groups", "col"), None, None),
            P(("groups", "col")),
            P(("groups", "col")),
            P(("groups", "col"), "row"),
            P(("groups", "col"), "row"),
        ),
        out_specs=(
            P(("groups", "col"), "row"),
            P(("groups", "col"), "row"),
            P(("groups", "col"), "row", None),
            P(("groups", "col"), "row", None),
        ),
        check_vma=False,
    )
```

```python
import jax
import jax.numpy as jnp
from jax import lax
from jax.experimental import pallas as pl
from jax.experimental.pallas import tpu as pltpu
from jax.sharding import PartitionSpec as P

TILE = 64
CHUNKS = 4


def product(left, right):
    return jnp.dot(left, right, precision=lax.Precision.HIGH, preferred_element_type=jnp.float32)


def product_t(left, right):
    return lax.dot_general(
        left,
        right,
        (((0,), (0,)), ((), ())),
        precision=lax.Precision.HIGH,
        preferred_element_type=jnp.float32,
    )


def batched(form, left, right):
    return jnp.einsum(
        form, left, right, precision=lax.Precision.HIGH, preferred_element_type=jnp.float32
    )


def masked_factors(panel_two_j, panel_two_r, inv_two, live, pattern_j, pattern_r):
    mask_j = jnp.repeat(pattern_j.astype(jnp.float32), TILE, axis=1)
    mask_r = jnp.repeat(pattern_r.astype(jnp.float32), TILE, axis=1)
    masked_j = panel_two_j * mask_j[:, :, None] * live[:, None, :]
    masked_r = panel_two_r * mask_r[:, :, None] * live[:, None, :]
    return batched("nak,nkm->nam", masked_j, inv_two), batched("nak,nkm->nam", masked_r, inv_two)


def live_columns(widths, width_two):
    return (jnp.arange(width_two)[None, :] < widths[:, None]).astype(jnp.float32)


def general_body(
    zroot,
    panel_one,
    inv_one,
    panel_two_j,
    panel_two_r,
    inv_two,
    parents,
    widths,
    pattern_j,
    pattern_r,
):
    rows = lax.axis_size("row")
    row = lax.axis_index("row")
    inverse = inv_one[0]
    width_one = inverse.shape[0]
    share_one = width_one // rows
    nodes, width_two = inv_two.shape[0], inv_two.shape[1]
    factor = product(panel_one[0], inverse)
    own_columns = lax.dynamic_slice_in_dim(inverse, row * share_one, share_one, 1)
    square = product_t(own_columns, inverse)
    factors = lax.all_gather(factor, "col", axis=0)
    squares_of = lax.all_gather(square, "col", axis=0)
    whole = lax.all_gather(factor, "row", axis=0, tiled=True)
    terms = jnp.sum(factor * product(zroot, whole), axis=0)
    var_one = jnp.sum(own_columns * own_columns, axis=0) + lax.psum_scatter(
        terms, "row", scatter_dimension=0, tiled=True
    )
    live = live_columns(widths, width_two)
    factor_j, factor_r = masked_factors(
        panel_two_j, panel_two_r, inv_two, live, pattern_j, pattern_r
    )
    whole_j = lax.all_gather(factor_j, "row", axis=1, tiled=True)
    parent = jnp.take(factors, parents, axis=0)
    parent_square = jnp.take(squares_of, parents, axis=0)
    head = batched("nab,nbm->nam", parent, whole_j) - factor_r
    whole_head = lax.all_gather(head, "row", axis=1, tiled=True)
    block_r = batched("ab,nbm->nam", zroot, whole_head)
    own_j = batched("nab,nbm->nam", parent_square, whole_j)
    block_j = -(
        own_j
        + lax.psum_scatter(
            batched("nab,nam->nbm", parent, block_r), "row", scatter_dimension=1, tiled=True
        )
    )
    terms_two = jnp.sum(head * block_r, axis=1) + jnp.sum(factor_j * own_j, axis=1)
    summed = lax.psum_scatter(terms_two, "row", scatter_dimension=1, tiled=True)
    share_two = summed.shape[1]
    squares = jnp.sum(inv_two * inv_two, axis=1)
    live_share = lax.dynamic_slice_in_dim(live, row * share_two, share_two, 1)
    square_share = lax.dynamic_slice_in_dim(squares, row * share_two, share_two, 1)
    return var_one[None, :], live_share * (square_share + summed), block_j, block_r


ACROSS = [(0, 2), (2, 0), (1, 3), (3, 1)]
SIBLING = [(0, 1), (1, 0), (2, 3), (3, 2)]


VMEM_LIMIT = 48 * 1024 * 1024
ANYWHERE = pl.BlockSpec(memory_space=pl.ANY)
SCALARS = pl.BlockSpec(memory_space=pltpu.SMEM)
WHOLE = pl.BlockSpec(memory_space=pltpu.VMEM)


def cost():
    return pl.CostEstimate(flops=1, bytes_accessed=1, transcendentals=0)


def params(**more):
    return pltpu.CompilerParams(vmem_limit_bytes=VMEM_LIMIT, **more)


def split(x):
    high = x.astype(jnp.bfloat16)
    return high, (x - high.astype(jnp.float32)).astype(jnp.bfloat16)


def three(left, right, contract=((1,), (0,))):
    def dot(a, b):
        return lax.dot_general(a, b, (contract, ((), ())), preferred_element_type=jnp.float32)

    return dot(left[0], right[0]) + (dot(left[0], right[1]) + dot(left[1], right[0]))


def level_one(panel, inverse, sizes):
    root_rows, width = panel.shape
    tile = 256
    starts = [sum(sizes[:q]) for q in range(len(sizes))]

    def kernel(panel_ref, inverse_ref, *refs):
        outs, (high, low) = refs[: len(sizes)], refs[len(sizes) :]

        @pl.when(pl.program_id(0) == 0)
        def _():
            high[...], low[...] = split(panel_ref[...])

        result = three((high[...], low[...]), split(inverse_ref[...]))
        for q, size in enumerate(sizes):
            outs[q][...] = result[starts[q] : starts[q] + size]

    return pl.pallas_call(
        kernel,
        grid=(width // tile,),
        in_specs=[
            pl.BlockSpec((root_rows, width), lambda i: (0, 0)),
            pl.BlockSpec((width, tile), lambda i: (0, i)),
        ],
        out_specs=[pl.BlockSpec((size, tile), lambda i: (0, i)) for size in sizes],
        out_shape=[jax.ShapeDtypeStruct((size, width), jnp.float32) for size in sizes],
        scratch_shapes=[pltpu.VMEM((root_rows, width), jnp.bfloat16)] * 2,
        compiler_params=params(),
        cost_estimate=cost(),
    )(panel, inverse)


def after(deps, *arrays):
    count = len(arrays)

    def kernel(*refs):
        outs = refs[count + len(deps) :]
        for k in range(count):
            outs[k][...] = refs[k][...]

    return pl.pallas_call(
        kernel,
        in_specs=[WHOLE] * count + [ANYWHERE] * len(deps),
        out_specs=[WHOLE] * count,
        out_shape=[jax.ShapeDtypeStruct(x.shape, x.dtype) for x in arrays],
        compiler_params=params(),
        cost_estimate=cost(),
    )(*arrays, *deps)


def square_rows(columns, inverse, deps):
    depth, share = columns.shape
    width = inverse.shape[1]
    tile = 256

    def kernel(columns_ref, inverse_ref, *refs):
        out_ref, high, low = refs[-3:]

        @pl.when(pl.program_id(0) == 0)
        def _():
            high[...], low[...] = split(columns_ref[...])

        out_ref[...] = three((high[...], low[...]), split(inverse_ref[...]), ((0,), (0,)))

    return pl.pallas_call(
        kernel,
        grid=(width // tile,),
        in_specs=[
            pl.BlockSpec((depth, share), lambda i: (0, 0)),
            pl.BlockSpec((depth, tile), lambda i: (0, i)),
        ]
        + [ANYWHERE] * len(deps),
        out_specs=pl.BlockSpec((share, tile), lambda i: (0, i)),
        out_shape=jax.ShapeDtypeStruct((share, width), jnp.float32),
        scratch_shapes=[pltpu.VMEM((depth, share), jnp.bfloat16)] * 2,
        compiler_params=params(),
        cost_estimate=cost(),
    )(columns, inverse, *deps)


def with_parent(parents, gathered, whole_j, minus, start, deps):
    nodes, depth, width = whole_j.shape
    part = gathered.shape[1]
    extra = [] if minus is None else [minus]

    def kernel(parents_ref, gathered_ref, whole_ref, *refs):
        out_ref, chosen_ref, sems = refs[-3:]

        def copy(n):
            return pltpu.make_async_copy(
                gathered_ref.at[parents_ref[n]], chosen_ref.at[n], sems.at[n]
            )

        for n in range(nodes):
            copy(n).start()
        for n in range(nodes):
            copy(n).wait()
            result = three(split(chosen_ref[n]), split(whole_ref[n]))
            if extra:
                result = result - refs[0][n, start : start + part, :]
            out_ref[:, n * width : (n + 1) * width] = result

    return pl.pallas_call(
        kernel,
        grid=(1,),
        in_specs=[SCALARS, ANYWHERE]
        + [pl.BlockSpec(x.shape, lambda i: (0, 0, 0)) for x in [whole_j] + extra]
        + [ANYWHERE] * len(deps),
        out_specs=[
            pl.BlockSpec((part, nodes * width), lambda i: (0, 0)),
            pl.BlockSpec((nodes, part, depth), lambda i: (0, 0, 0)),
        ],
        out_shape=[
            jax.ShapeDtypeStruct((part, nodes * width), jnp.float32),
            jax.ShapeDtypeStruct((nodes, part, depth), jnp.float32),
        ],
        scratch_shapes=[pltpu.SemaphoreType.DMA((nodes,))],
        compiler_params=params(),
        cost_estimate=cost(),
    )(parents, gathered, whole_j, *extra, *deps)


def in_order(order, blocks, deps):
    nodes, share, width = blocks[0].shape
    count = len(blocks)

    def kernel(order_ref, *refs):
        out_ref = refs[-1]
        for k in range(count):
            start = pl.multiple_of(order_ref[k] * share, share)
            for n in range(nodes):
                out_ref[n, pl.ds(start, share), :] = refs[k][n]

    return pl.pallas_call(
        kernel,
        in_specs=[SCALARS] + [WHOLE] * count + [ANYWHERE] * len(deps),
        out_specs=WHOLE,
        out_shape=jax.ShapeDtypeStruct((nodes, count * share, width), jnp.float32),
        compiler_params=params(),
        cost_estimate=cost(),
    )(order, *blocks, *deps)


def halves_of(place, own, deps):
    width = own[0].shape[1]
    half = width // 2
    starts = [sum(x.shape[0] for x in own[:q]) for q in range(len(own))]
    rows = sum(x.shape[0] for x in own)

    def kernel(place_ref, *refs):
        outs = refs[len(own) + len(deps) :]
        for k in range(2):
            at = pl.ds(pl.multiple_of((1 - place_ref[k]) * half, half), half)
            for q, x in enumerate(own):
                outs[k][starts[q] : starts[q] + x.shape[0], :] = refs[q][:, at]

    return pl.pallas_call(
        kernel,
        in_specs=[SCALARS] + [WHOLE] * len(own) + [ANYWHERE] * len(deps),
        out_specs=[WHOLE] * 2,
        out_shape=[jax.ShapeDtypeStruct((rows, half), jnp.float32)] * 2,
        compiler_params=params(),
        cost_estimate=cost(),
    )(place, *own, *deps)


def pair_terms(heads, block_r, deps):
    nodes, _, width = block_r.shape
    starts = [sum(x.shape[0] for x in heads[:q]) for q in range(len(heads))]

    def kernel(*refs):
        block_ref, out_ref = refs[len(heads)], refs[-1]
        for n in range(nodes):
            total = jnp.zeros((1, width), jnp.float32)
            for q, head in enumerate(heads):
                total = total + jnp.sum(
                    refs[q][:, n * width : (n + 1) * width]
                    * block_ref[n, starts[q] : starts[q] + head.shape[0], :],
                    axis=0,
                    keepdims=True,
                )
            out_ref[n : n + 1, :] = total

    return pl.pallas_call(
        kernel,
        in_specs=[WHOLE] * (len(heads) + 1) + [ANYWHERE] * len(deps),
        out_specs=WHOLE,
        out_shape=jax.ShapeDtypeStruct((nodes, width), jnp.float32),
        compiler_params=params(),
        cost_estimate=cost(),
    )(*heads, block_r, *deps)


def root_terms(place, zroot, own, sibling, across_same, across_other, deps):
    root_rows = zroot.shape[0]
    width = own[0].shape[1]
    half = width // 2
    count = len(own)
    starts = [sum(x.shape[0] for x in own[:q]) for q in range(count)]

    def kernel(place_ref, root_ref, *refs):
        sibling_ref, same_ref, other_ref = refs[count : count + 3]
        out_ref, factor = refs[-2:]
        chip, core = place_ref[0], place_ref[1]
        for q, x in enumerate(own):
            factor[starts[q] : starts[q] + x.shape[0], :] = refs[q][...]

        def root(which):
            start = pl.multiple_of(which * root_rows, root_rows)
            return split(root_ref[:, pl.ds(start, root_rows)])

        def halved(which):
            return factor[:, pl.ds(pl.multiple_of(which * half, half), half)]

        def put(which, value):
            at = pl.ds(pl.multiple_of(which * half, half), half)
            out_ref[:, at] = out_ref[:, at] + 2 * jnp.sum(value, axis=0, keepdims=True)

        out_ref[...] = jnp.sum(
            factor[...] * three(root(2 * chip + core), split(factor[...])), axis=0, keepdims=True
        )
        put(core, halved(core) * three(root(2 * chip + 1 - core), split(sibling_ref[...])))
        put(
            chip,
            halved(chip)
            * (
                three(root(2 * (1 - chip) + core), split(same_ref[...]))
                + three(root(2 * (1 - chip) + 1 - core), split(other_ref[...]))
            ),
        )

    return pl.pallas_call(
        kernel,
        in_specs=[SCALARS] + [WHOLE] * (1 + count + 3) + [ANYWHERE] * len(deps),
        out_specs=WHOLE,
        out_shape=jax.ShapeDtypeStruct((1, width), jnp.float32),
        scratch_shapes=[pltpu.VMEM((root_rows, width), jnp.float32)],
        compiler_params=params(),
        cost_estimate=cost(),
    )(place, zroot, *own, sibling, across_same, across_other, *deps)


def root_step(order, zroot, start, parts, before, nodes, deps):
    root_rows = zroot.shape[0]
    size, columns = parts[0].shape
    width = columns // nodes
    count = len(parts)
    tile = 256
    tiles = width // tile
    extra = [] if before is None else [before]

    def kernel(order_ref, root_ref, *refs):
        out_ref, root, high, low, head_high, head_low, sems = refs[-7:]

        @pl.when(pl.program_id(0) == 0)
        def _():
            copies = []
            for k in range(count):
                at = pl.ds(pl.multiple_of(order_ref[k] * root_rows + start, 128), size)
                copies.append(pltpu.make_async_copy(root_ref.at[:, at], root.at[k], sems.at[k]))
                copies[k].start()
            for k in range(count):
                at = slice(k * size, (k + 1) * size)
                copies[k].wait()
                high[:, at], low[:, at] = split(root[k])

        for k in range(count):
            at = slice(k * size, (k + 1) * size)
            head_high[at, :], head_low[at, :] = split(refs[k][...])
        result = three((high[...], low[...]), (head_high[...], head_low[...]))
        out_ref[...] = result + refs[count][...] if extra else result

    block = pl.BlockSpec((None, root_rows, tile), lambda i: (i // tiles, 0, i % tiles))
    return pl.pallas_call(
        kernel,
        grid=(nodes * tiles,),
        in_specs=[SCALARS, ANYWHERE]
        + [pl.BlockSpec((size, tile), lambda i: (0, i))] * count
        + [block] * len(extra)
        + [ANYWHERE] * len(deps),
        out_specs=block,
        out_shape=jax.ShapeDtypeStruct((nodes, root_rows, width), jnp.float32),
        scratch_shapes=[pltpu.VMEM((count, root_rows, size), jnp.float32)]
        + [pltpu.VMEM((root_rows, count * size), jnp.bfloat16)] * 2
        + [pltpu.VMEM((count * size, tile), jnp.bfloat16)] * 2
        + [pltpu.SemaphoreType.DMA((count,))],
        compiler_params=params(),
        cost_estimate=cost(),
    )(order, zroot, *parts, *extra, *deps)


def transposed(which, taken, node, block_r, deps):
    depth = taken[0].shape[2]
    _, rows, width = block_r.shape
    share = depth // 4
    count = len(taken)
    starts = [sum(x.shape[1] for x in taken[:q]) for q in range(count)]

    def kernel(which_ref, *refs):
        block_ref = refs[count]
        out_ref, left = refs[-2:]
        for q, x in enumerate(taken):
            for chip in range(2):
                start = pl.multiple_of((2 * chip + which_ref[0]) * share, share)
                left[
                    starts[q] : starts[q] + x.shape[1], chip * share : (chip + 1) * share
                ] = refs[q][:, pl.ds(start, share)]
        out_ref[...] = three(split(left[...]), split(block_ref[...]), ((0,), (0,)))

    return pl.pallas_call(
        kernel,
        grid=(1,),
        in_specs=[SCALARS]
        + [pl.BlockSpec((None,) + x.shape[1:], lambda i: (node, 0, 0)) for x in taken]
        + [pl.BlockSpec((None, rows, width), lambda i: (node, 0, 0))]
        + [ANYWHERE] * len(deps),
        out_specs=pl.BlockSpec((2 * share, width), lambda i: (0, 0)),
        out_shape=jax.ShapeDtypeStruct((2 * share, width), jnp.float32),
        scratch_shapes=[pltpu.VMEM((rows, 2 * share), jnp.float32)],
        compiler_params=params(),
        cost_estimate=cost(),
    )(which, *taken, block_r, *deps)


def halved_sums(chip, kept, received, deps):
    nodes = len(kept)
    rows, width = kept[0].shape
    share = rows // 2

    def kernel(chip_ref, *refs):
        theirs_ref, mine_ref = refs[-2:]
        for out_ref, which in ((theirs_ref, 1 - chip_ref[0]), (mine_ref, chip_ref[0])):
            at = pl.ds(pl.multiple_of(which * share, share), share)
            for n in range(nodes):
                out_ref[n] = refs[n][at, :] + refs[nodes + n][at, :]

    return pl.pallas_call(
        kernel,
        in_specs=[SCALARS] + [WHOLE] * (2 * nodes) + [ANYWHERE] * len(deps),
        out_specs=[WHOLE] * 2,
        out_shape=[jax.ShapeDtypeStruct((nodes, share, width), jnp.float32)] * 2,
        compiler_params=params(),
        cost_estimate=cost(),
    )(chip, *kept, *received, *deps)


def line_body(
    zroot,
    panel_one,
    inv_one,
    panel_two_j,
    panel_two_r,
    inv_two,
    parents,
    widths,
    pattern_j,
    pattern_r,
):
    rows, cols = 4, 4
    row = lax.axis_index("row")
    col = lax.axis_index("col")
    chip, core = row // 2, row % 2
    root_rows = zroot.shape[0]
    inverse = inv_one[0]
    width_one = inverse.shape[0]
    share_one = width_one // rows
    nodes, width_two = inv_two.shape[0], inv_two.shape[1]

    here = jnp.stack([chip, core]).astype(jnp.int32)

    order = jnp.stack([row, row ^ 1, row ^ 2, row ^ 3]).astype(jnp.int32)
    chain = []

    def exchange(x):
        across = lax.ppermute(x, "row", ACROSS)
        beside = lax.ppermute(x, "row", SIBLING)
        return [x, beside, across, lax.ppermute(across, "row", SIBLING)]

    sizes = [root_rows - root_rows // 4, root_rows // 4]
    starts = [0, sizes[0]]
    own = list(level_one(panel_one[0], inverse, sizes))
    gathered = [lax.all_gather(x, "col", axis=0) for x in own]
    own_columns = lax.dynamic_slice_in_dim(inverse, row * share_one, share_one, 1)
    square = square_rows(own_columns, inverse, [own[0]])
    chain.append([square])

    live = live_columns(widths, width_two)
    factor_j, factor_r = masked_factors(
        panel_two_j, panel_two_r, inv_two, live, pattern_j, pattern_r
    )
    shares_j = exchange(factor_j)
    whole_j = in_order(order, shares_j, chain[-1])
    chain.append([whole_j])
    to_chip, to_core = halves_of(here, own, chain[-1])
    chain.append([to_chip])
    across_same = lax.ppermute(to_chip, "row", ACROSS)
    across_other = lax.ppermute(across_same, "row", SIBLING)
    sibling = lax.ppermute(to_core, "row", SIBLING)

    heads, taken = [], []
    parents_here = parents.astype(jnp.int32)

    def parent_step(q):
        out, chosen = with_parent(
            parents_here, gathered[q], whole_j, factor_r, starts[q], chain[-1]
        )
        heads.append(out)
        taken.append(chosen)
        chain.append([out])
        return out

    def gather_step(q, parts, before):
        out = root_step(order, zroot, starts[q], parts, before, nodes, chain[-1])
        chain.append([out])
        return out

    terms_one = root_terms(here, zroot, own, sibling, across_same, across_other, chain[-1])
    chain.append([terms_one])
    early = exchange(parent_step(0))
    (square,) = after(chain[-1], square)
    squares_of = lax.all_gather(square, "col", axis=0)
    late = parent_step(1)
    late_across = lax.ppermute(late, "row", ACROSS)
    late_beside = lax.ppermute(late, "row", SIBLING)
    block_r = gather_step(0, early, None)
    (late_across,) = after(chain[-1], late_across)
    late_other = lax.ppermute(late_across, "row", SIBLING)
    block_r = gather_step(1, [late, late_beside, late_across, late_other], block_r)
    received, kept = [], []
    for n in range(nodes):
        which = (1 - core)[None].astype(jnp.int32)
        sent = transposed(which, taken, n, block_r, chain[-1])
        received.append(lax.ppermute(sent, "row", SIBLING))
        chain.append([sent])
    for n in range(nodes):
        which = core[None].astype(jnp.int32)
        keep = transposed(which, taken, n, block_r, chain[-1])
        kept.append(keep)
        chain.append([keep])
    theirs, mine = halved_sums(here, kept, received, chain[-1])
    chain.append([mine])
    sums = mine + lax.ppermute(theirs, "row", ACROSS)
    pairs = pair_terms(heads, block_r, chain[-1])
    chain.append([pairs])
    own_rows, _ = with_parent(parents_here, squares_of, whole_j, None, 0, chain[-1])
    blocks_j, terms_two = [], []
    for n in range(nodes):
        own_j = own_rows[:, n * width_two : (n + 1) * width_two]
        blocks_j.append(-(own_j + sums[n]))
        terms_two.append(pairs[n] + jnp.sum(factor_j[n] * own_j, axis=0))
    block_j = jnp.stack(blocks_j)

    share_two = width_two // rows
    packed = jnp.concatenate(
        [terms_one.reshape(rows, share_one)] + [t.reshape(rows, share_two) for t in terms_two],
        axis=1,
    ).reshape(2, 2, -1)
    packed = lax.dynamic_index_in_dim(packed, core, 1, keepdims=False) + lax.ppermute(
        lax.dynamic_index_in_dim(packed, 1 - core, 1, keepdims=False), "row", SIBLING
    )
    packed = lax.dynamic_index_in_dim(packed, chip, 0, keepdims=False) + lax.ppermute(
        lax.dynamic_index_in_dim(packed, 1 - chip, 0, keepdims=False), "row", ACROSS
    )
    var_one = packed[:share_one] + jnp.sum(own_columns * own_columns, axis=0)
    squares = jnp.sum(inv_two * inv_two, axis=1)
    live_share = lax.dynamic_slice_in_dim(live, row * share_two, share_two, 1)
    square_share = lax.dynamic_slice_in_dim(squares, row * share_two, share_two, 1)
    var_two = live_share * (square_share + packed[share_one:].reshape(nodes, share_two))
    return var_one[None, :], var_two, block_j, block_r


def solution(mesh):
    line = mesh.shape["row"] == 4 and mesh.shape["col"] == 4

    def body(*args):
        two_nodes = args[5].shape[0] == 2
        return (line_body if line and two_nodes else general_body)(*args)

    return jax.shard_map(
        body,
        mesh=mesh,
        in_specs=(
            P(("groups", "row"), None),
            P(("groups", "col"), "row", None),
            P(("groups", "col"), None, None),
            P(("groups", "col"), "row", None),
            P(("groups", "col"), "row", None),
            P(("groups", "col"), None, None),
            P(("groups", "col")),
            P(("groups", "col")),
            P(("groups", "col"), "row"),
            P(("groups", "col"), "row"),
        ),
        out_specs=(
            P(("groups", "col"), "row"),
            P(("groups", "col"), "row"),
            P(("groups", "col"), "row", None),
            P(("groups", "col"), "row", None),
        ),
        check_vma=False,
    )
```

```python
import jax
import jax.numpy as jnp
from jax import lax
from jax.experimental import pallas as pl
from jax.experimental.pallas import tpu as pltpu
from jax.sharding import PartitionSpec as P

TILE = 64
CHUNKS = 4


def product(left, right):
    return jnp.dot(left, right, precision=lax.Precision.HIGH, preferred_element_type=jnp.float32)


def product_t(left, right):
    return lax.dot_general(
        left,
        right,
        (((0,), (0,)), ((), ())),
        precision=lax.Precision.HIGH,
        preferred_element_type=jnp.float32,
    )


def batched(form, left, right):
    return jnp.einsum(
        form, left, right, precision=lax.Precision.HIGH, preferred_element_type=jnp.float32
    )


def masked_factors(panel_two_j, panel_two_r, inv_two, live, pattern_j, pattern_r):
    mask_j = jnp.repeat(pattern_j.astype(jnp.float32), TILE, axis=1)
    mask_r = jnp.repeat(pattern_r.astype(jnp.float32), TILE, axis=1)
    masked_j = panel_two_j * mask_j[:, :, None] * live[:, None, :]
    masked_r = panel_two_r * mask_r[:, :, None] * live[:, None, :]
    return batched("nak,nkm->nam", masked_j, inv_two), batched("nak,nkm->nam", masked_r, inv_two)


def live_columns(widths, width_two):
    return (jnp.arange(width_two)[None, :] < widths[:, None]).astype(jnp.float32)


def general_body(
    zroot,
    panel_one,
    inv_one,
    panel_two_j,
    panel_two_r,
    inv_two,
    parents,
    widths,
    pattern_j,
    pattern_r,
):
    rows = lax.axis_size("row")
    row = lax.axis_index("row")
    inverse = inv_one[0]
    width_one = inverse.shape[0]
    share_one = width_one // rows
    nodes, width_two = inv_two.shape[0], inv_two.shape[1]
    factor = product(panel_one[0], inverse)
    own_columns = lax.dynamic_slice_in_dim(inverse, row * share_one, share_one, 1)
    square = product_t(own_columns, inverse)
    factors = lax.all_gather(factor, "col", axis=0)
    squares_of = lax.all_gather(square, "col", axis=0)
    whole = lax.all_gather(factor, "row", axis=0, tiled=True)
    terms = jnp.sum(factor * product(zroot, whole), axis=0)
    var_one = jnp.sum(own_columns * own_columns, axis=0) + lax.psum_scatter(
        terms, "row", scatter_dimension=0, tiled=True
    )
    live = live_columns(widths, width_two)
    factor_j, factor_r = masked_factors(
        panel_two_j, panel_two_r, inv_two, live, pattern_j, pattern_r
    )
    whole_j = lax.all_gather(factor_j, "row", axis=1, tiled=True)
    parent = jnp.take(factors, parents, axis=0)
    parent_square = jnp.take(squares_of, parents, axis=0)
    head = batched("nab,nbm->nam", parent, whole_j) - factor_r
    whole_head = lax.all_gather(head, "row", axis=1, tiled=True)
    block_r = batched("ab,nbm->nam", zroot, whole_head)
    own_j = batched("nab,nbm->nam", parent_square, whole_j)
    block_j = -(
        own_j
        + lax.psum_scatter(
            batched("nab,nam->nbm", parent, block_r), "row", scatter_dimension=1, tiled=True
        )
    )
    terms_two = jnp.sum(head * block_r, axis=1) + jnp.sum(factor_j * own_j, axis=1)
    summed = lax.psum_scatter(terms_two, "row", scatter_dimension=1, tiled=True)
    share_two = summed.shape[1]
    squares = jnp.sum(inv_two * inv_two, axis=1)
    live_share = lax.dynamic_slice_in_dim(live, row * share_two, share_two, 1)
    square_share = lax.dynamic_slice_in_dim(squares, row * share_two, share_two, 1)
    return var_one[None, :], live_share * (square_share + summed), block_j, block_r


ACROSS = [(0, 2), (2, 0), (1, 3), (3, 1)]
SIBLING = [(0, 1), (1, 0), (2, 3), (3, 2)]


CHUNKS = 4
VMEM_LIMIT = 48 * 1024 * 1024
ANYWHERE = pl.BlockSpec(memory_space=pl.ANY)
SCALARS = pl.BlockSpec(memory_space=pltpu.SMEM)
WHOLE = pl.BlockSpec(memory_space=pltpu.VMEM)


def cost():
    return pl.CostEstimate(flops=1, bytes_accessed=1, transcendentals=0)


def params(**more):
    return pltpu.CompilerParams(vmem_limit_bytes=VMEM_LIMIT, **more)


def split(x):
    high = x.astype(jnp.bfloat16)
    return high, (x - high.astype(jnp.float32)).astype(jnp.bfloat16)


def three(left, right, contract=((1,), (0,))):
    def dot(a, b):
        return lax.dot_general(a, b, (contract, ((), ())), preferred_element_type=jnp.float32)

    return dot(left[0], right[0]) + (dot(left[0], right[1]) + dot(left[1], right[0]))


def level_one(panel, inverse, sizes):
    root_rows, width = panel.shape
    tile = 256
    starts = [sum(sizes[:q]) for q in range(len(sizes))]

    def kernel(panel_ref, inverse_ref, *refs):
        outs, (high, low) = refs[: len(sizes)], refs[len(sizes) :]

        @pl.when(pl.program_id(0) == 0)
        def _():
            high[...], low[...] = split(panel_ref[...])

        result = three((high[...], low[...]), split(inverse_ref[...]))
        for q, size in enumerate(sizes):
            outs[q][...] = result[starts[q] : starts[q] + size]

    return pl.pallas_call(
        kernel,
        grid=(width // tile,),
        in_specs=[
            pl.BlockSpec((root_rows, width), lambda i: (0, 0)),
            pl.BlockSpec((width, tile), lambda i: (0, i)),
        ],
        out_specs=[pl.BlockSpec((size, tile), lambda i: (0, i)) for size in sizes],
        out_shape=[jax.ShapeDtypeStruct((size, width), jnp.float32) for size in sizes],
        scratch_shapes=[pltpu.VMEM((root_rows, width), jnp.bfloat16)] * 2,
        compiler_params=params(),
        cost_estimate=cost(),
    )(panel, inverse)


def after(deps, *arrays):
    count = len(arrays)

    def kernel(*refs):
        outs = refs[count + len(deps) :]
        for k in range(count):
            outs[k][...] = refs[k][...]

    return pl.pallas_call(
        kernel,
        in_specs=[WHOLE] * count + [ANYWHERE] * len(deps),
        out_specs=[WHOLE] * count,
        out_shape=[jax.ShapeDtypeStruct(x.shape, x.dtype) for x in arrays],
        compiler_params=params(),
        cost_estimate=cost(),
    )(*arrays, *deps)


def square_rows(columns, inverse, deps):
    depth, share = columns.shape
    width = inverse.shape[1]
    tile = 256

    def kernel(columns_ref, inverse_ref, *refs):
        out_ref, high, low = refs[-3:]

        @pl.when(pl.program_id(0) == 0)
        def _():
            high[...], low[...] = split(columns_ref[...])

        out_ref[...] = three((high[...], low[...]), split(inverse_ref[...]), ((0,), (0,)))

    return pl.pallas_call(
        kernel,
        grid=(width // tile,),
        in_specs=[
            pl.BlockSpec((depth, share), lambda i: (0, 0)),
            pl.BlockSpec((depth, tile), lambda i: (0, i)),
        ]
        + [ANYWHERE] * len(deps),
        out_specs=pl.BlockSpec((share, tile), lambda i: (0, i)),
        out_shape=jax.ShapeDtypeStruct((share, width), jnp.float32),
        scratch_shapes=[pltpu.VMEM((depth, share), jnp.bfloat16)] * 2,
        compiler_params=params(),
        cost_estimate=cost(),
    )(columns, inverse, *deps)


def with_parent(choice, rotated, whole_j, minus, start, deps):
    nodes, depth, width = whole_j.shape
    part = rotated[0].shape[0]
    count = len(rotated)
    extra = [] if minus is None else [minus]

    def kernel(choice_ref, *refs):
        whole_ref = refs[count]
        out_ref, chosen_ref, sems = refs[-3:]
        for n in range(nodes):
            for k in range(count):

                @pl.when(choice_ref[n] == k)
                def _():
                    pltpu.make_async_copy(refs[k], chosen_ref.at[n], sems.at[n]).start()

        for n in range(nodes):
            pltpu.make_async_copy(refs[0], chosen_ref.at[n], sems.at[n]).wait()
            result = three(split(chosen_ref[n]), split(whole_ref[n]))
            if extra:
                result = result - refs[count + 1][n, start : start + part, :]
            out_ref[:, n * width : (n + 1) * width] = result

    return pl.pallas_call(
        kernel,
        grid=(1,),
        in_specs=[SCALARS]
        + [ANYWHERE] * count
        + [pl.BlockSpec(x.shape, lambda i: (0, 0, 0)) for x in [whole_j] + extra]
        + [ANYWHERE] * len(deps),
        out_specs=[
            pl.BlockSpec((part, nodes * width), lambda i: (0, 0)),
            pl.BlockSpec((nodes, part, depth), lambda i: (0, 0, 0)),
        ],
        out_shape=[
            jax.ShapeDtypeStruct((part, nodes * width), jnp.float32),
            jax.ShapeDtypeStruct((nodes, part, depth), jnp.float32),
        ],
        scratch_shapes=[pltpu.SemaphoreType.DMA((nodes,))],
        compiler_params=params(),
        cost_estimate=cost(),
    )(choice, *rotated, whole_j, *extra, *deps)


def in_order(order, blocks, deps):
    nodes, share, width = blocks[0].shape
    count = len(blocks)

    def kernel(order_ref, *refs):
        out_ref = refs[-1]
        for k in range(count):
            start = pl.multiple_of(order_ref[k] * share, share)
            for n in range(nodes):
                out_ref[n, pl.ds(start, share), :] = refs[k][n]

    return pl.pallas_call(
        kernel,
        in_specs=[SCALARS] + [WHOLE] * count + [ANYWHERE] * len(deps),
        out_specs=WHOLE,
        out_shape=jax.ShapeDtypeStruct((nodes, count * share, width), jnp.float32),
        compiler_params=params(),
        cost_estimate=cost(),
    )(order, *blocks, *deps)


def halves_of(place, own, deps):
    width = own[0].shape[1]
    half = width // 2
    starts = [sum(x.shape[0] for x in own[:q]) for q in range(len(own))]
    rows = sum(x.shape[0] for x in own)

    def kernel(place_ref, *refs):
        outs = refs[len(own) + len(deps) :]
        for k in range(2):
            at = pl.ds(pl.multiple_of((1 - place_ref[k]) * half, half), half)
            for q, x in enumerate(own):
                outs[k][starts[q] : starts[q] + x.shape[0], :] = refs[q][:, at]

    return pl.pallas_call(
        kernel,
        in_specs=[SCALARS] + [WHOLE] * len(own) + [ANYWHERE] * len(deps),
        out_specs=[WHOLE] * 2,
        out_shape=[jax.ShapeDtypeStruct((rows, half), jnp.float32)] * 2,
        compiler_params=params(),
        cost_estimate=cost(),
    )(place, *own, *deps)


def pair_terms(heads, block_r, deps):
    nodes, _, width = block_r.shape
    starts = [sum(x.shape[0] for x in heads[:q]) for q in range(len(heads))]

    def kernel(*refs):
        block_ref, out_ref = refs[len(heads)], refs[-1]
        for n in range(nodes):
            total = jnp.zeros((1, width), jnp.float32)
            for q, head in enumerate(heads):
                total = total + jnp.sum(
                    refs[q][:, n * width : (n + 1) * width]
                    * block_ref[n, starts[q] : starts[q] + head.shape[0], :],
                    axis=0,
                    keepdims=True,
                )
            out_ref[n : n + 1, :] = total

    return pl.pallas_call(
        kernel,
        in_specs=[WHOLE] * (len(heads) + 1) + [ANYWHERE] * len(deps),
        out_specs=WHOLE,
        out_shape=jax.ShapeDtypeStruct((nodes, width), jnp.float32),
        compiler_params=params(),
        cost_estimate=cost(),
    )(*heads, block_r, *deps)


def root_terms(place, zroot, own, sibling, across_same, across_other, deps):
    root_rows = zroot.shape[0]
    width = own[0].shape[1]
    half = width // 2
    count = len(own)
    starts = [sum(x.shape[0] for x in own[:q]) for q in range(count)]

    def kernel(place_ref, root_ref, *refs):
        sibling_ref, same_ref, other_ref = refs[count : count + 3]
        out_ref, factor = refs[-2:]
        chip, core = place_ref[0], place_ref[1]
        for q, x in enumerate(own):
            factor[starts[q] : starts[q] + x.shape[0], :] = refs[q][...]

        def root(which):
            start = pl.multiple_of(which * root_rows, root_rows)
            return split(root_ref[:, pl.ds(start, root_rows)])

        def halved(which):
            return factor[:, pl.ds(pl.multiple_of(which * half, half), half)]

        def put(which, value):
            at = pl.ds(pl.multiple_of(which * half, half), half)
            out_ref[:, at] = out_ref[:, at] + 2 * jnp.sum(value, axis=0, keepdims=True)

        out_ref[...] = jnp.sum(
            factor[...] * three(root(2 * chip + core), split(factor[...])), axis=0, keepdims=True
        )
        put(core, halved(core) * three(root(2 * chip + 1 - core), split(sibling_ref[...])))
        put(
            chip,
            halved(chip)
            * (
                three(root(2 * (1 - chip) + core), split(same_ref[...]))
                + three(root(2 * (1 - chip) + 1 - core), split(other_ref[...]))
            ),
        )

    return pl.pallas_call(
        kernel,
        in_specs=[SCALARS] + [WHOLE] * (1 + count + 3) + [ANYWHERE] * len(deps),
        out_specs=WHOLE,
        out_shape=jax.ShapeDtypeStruct((1, width), jnp.float32),
        scratch_shapes=[pltpu.VMEM((root_rows, width), jnp.float32)],
        compiler_params=params(),
        cost_estimate=cost(),
    )(place, zroot, *own, sibling, across_same, across_other, *deps)


def root_step(order, zroot, start, parts, before, nodes, deps):
    root_rows = zroot.shape[0]
    size, columns = parts[0].shape
    width = columns // nodes
    count = len(parts)
    tile = 256
    tiles = width // tile
    extra = [] if before is None else [before]

    def kernel(order_ref, root_ref, *refs):
        out_ref, root, high, low, head_high, head_low, sems = refs[-7:]

        @pl.when(pl.program_id(0) == 0)
        def _():
            copies = []
            for k in range(count):
                at = pl.ds(pl.multiple_of(order_ref[k] * root_rows + start, 128), size)
                copies.append(pltpu.make_async_copy(root_ref.at[:, at], root.at[k], sems.at[k]))
                copies[k].start()
            for k in range(count):
                at = slice(k * size, (k + 1) * size)
                copies[k].wait()
                high[:, at], low[:, at] = split(root[k])

        for k in range(count):
            at = slice(k * size, (k + 1) * size)
            head_high[at, :], head_low[at, :] = split(refs[k][...])
        result = three((high[...], low[...]), (head_high[...], head_low[...]))
        out_ref[...] = result + refs[count][...] if extra else result

    block = pl.BlockSpec((None, root_rows, tile), lambda i: (i // tiles, 0, i % tiles))
    return pl.pallas_call(
        kernel,
        grid=(nodes * tiles,),
        in_specs=[SCALARS, ANYWHERE]
        + [pl.BlockSpec((size, tile), lambda i: (0, i))] * count
        + [block] * len(extra)
        + [ANYWHERE] * len(deps),
        out_specs=block,
        out_shape=jax.ShapeDtypeStruct((nodes, root_rows, width), jnp.float32),
        scratch_shapes=[pltpu.VMEM((count, root_rows, size), jnp.float32)]
        + [pltpu.VMEM((root_rows, count * size), jnp.bfloat16)] * 2
        + [pltpu.VMEM((count * size, tile), jnp.bfloat16)] * 2
        + [pltpu.SemaphoreType.DMA((count,))],
        compiler_params=params(),
        cost_estimate=cost(),
    )(order, zroot, *parts, *extra, *deps)


def transposed(which, taken, node, block_r, deps):
    depth = taken[0].shape[2]
    _, rows, width = block_r.shape
    share = depth // 4
    count = len(taken)
    starts = [sum(x.shape[1] for x in taken[:q]) for q in range(count)]

    def kernel(which_ref, *refs):
        block_ref = refs[count]
        out_ref, left = refs[-2:]
        for q, x in enumerate(taken):
            for chip in range(2):
                start = pl.multiple_of((2 * chip + which_ref[0]) * share, share)
                left[
                    starts[q] : starts[q] + x.shape[1], chip * share : (chip + 1) * share
                ] = refs[q][:, pl.ds(start, share)]
        out_ref[...] = three(split(left[...]), split(block_ref[...]), ((0,), (0,)))

    return pl.pallas_call(
        kernel,
        grid=(1,),
        in_specs=[SCALARS]
        + [pl.BlockSpec((None,) + x.shape[1:], lambda i: (node, 0, 0)) for x in taken]
        + [pl.BlockSpec((None, rows, width), lambda i: (node, 0, 0))]
        + [ANYWHERE] * len(deps),
        out_specs=pl.BlockSpec((2 * share, width), lambda i: (0, 0)),
        out_shape=jax.ShapeDtypeStruct((2 * share, width), jnp.float32),
        scratch_shapes=[pltpu.VMEM((rows, 2 * share), jnp.float32)],
        compiler_params=params(),
        cost_estimate=cost(),
    )(which, *taken, block_r, *deps)


def halved_sums(chip, kept, received, deps):
    nodes = len(kept)
    rows, width = kept[0].shape
    share = rows // 2

    def kernel(chip_ref, *refs):
        theirs_ref, mine_ref = refs[-2:]
        for out_ref, which in ((theirs_ref, 1 - chip_ref[0]), (mine_ref, chip_ref[0])):
            at = pl.ds(pl.multiple_of(which * share, share), share)
            for n in range(nodes):
                out_ref[n] = refs[n][at, :] + refs[nodes + n][at, :]

    return pl.pallas_call(
        kernel,
        in_specs=[SCALARS] + [WHOLE] * (2 * nodes) + [ANYWHERE] * len(deps),
        out_specs=[WHOLE] * 2,
        out_shape=[jax.ShapeDtypeStruct((nodes, share, width), jnp.float32)] * 2,
        compiler_params=params(),
        cost_estimate=cost(),
    )(chip, *kept, *received, *deps)


def line_body(
    zroot,
    panel_one,
    inv_one,
    panel_two_j,
    panel_two_r,
    inv_two,
    parents,
    widths,
    pattern_j,
    pattern_r,
):
    rows, cols = 4, 4
    row = lax.axis_index("row")
    col = lax.axis_index("col")
    chip, core = row // 2, row % 2
    root_rows = zroot.shape[0]
    inverse = inv_one[0]
    width_one = inverse.shape[0]
    share_one = width_one // rows
    nodes, width_two = inv_two.shape[0], inv_two.shape[1]

    here = jnp.stack([chip, core]).astype(jnp.int32)

    order = jnp.stack([row, row ^ 1, row ^ 2, row ^ 3]).astype(jnp.int32)
    chain = []

    def exchange(x):
        across = lax.ppermute(x, "row", ACROSS)
        beside = lax.ppermute(x, "row", SIBLING)
        return [x, beside, across, lax.ppermute(across, "row", SIBLING)]

    def turn(x):
        return lax.ppermute(x, "col", [(i, (i + 1) % cols) for i in range(cols)])

    size = root_rows // CHUNKS
    starts = [q * size for q in range(CHUNKS)]
    own = list(level_one(panel_one[0], inverse, [size] * CHUNKS))
    rounds = [own]
    rounds.append([turn(x) for x in own])

    live = live_columns(widths, width_two)
    factor_j, factor_r = masked_factors(
        panel_two_j, panel_two_r, inv_two, live, pattern_j, pattern_r
    )
    (factor_j,) = after([own[0]], factor_j)
    across_j = lax.ppermute(factor_j, "row", ACROSS)
    beside_j = lax.ppermute(factor_j, "row", SIBLING)
    own_columns = lax.dynamic_slice_in_dim(inverse, row * share_one, share_one, 1)
    square = square_rows(own_columns, inverse, [factor_j])
    half = CHUNKS // 2
    (across_j,) = after(rounds[1][:half] + [square, factor_r], across_j)
    other_j = lax.ppermute(across_j, "row", SIBLING)
    to_chip, to_core = halves_of(here, own, [across_j])
    across_same = lax.ppermute(to_chip, "row", ACROSS)
    sibling = lax.ppermute(to_core, "row", SIBLING)
    whole_j = in_order(
        order, [factor_j, beside_j, across_j, other_j], rounds[1][half:] + [to_chip]
    )
    rounds.append([turn(x) for x in rounds[1]])
    (across_same,) = after(rounds[2] + [whole_j, sibling], across_same)
    chain.append([across_same])
    rounds.append([turn(x) for x in rounds[2]])
    across_other = lax.ppermute(across_same, "row", SIBLING)

    heads, taken, wholes = [], [], []
    choice = ((col - parents) % cols).astype(jnp.int32)

    def parent_step(q):
        out, chosen = with_parent(
            choice, [r[q] for r in rounds], whole_j, factor_r, starts[q], chain[-1]
        )
        heads.append(out)
        taken.append(chosen)
        wholes.append(exchange(out) if q < CHUNKS - 1 else None)
        chain.append([out])
        return out

    def gather_step(q, before):
        out = root_step(order, zroot, starts[q], wholes[q], before, nodes, chain[-1])
        chain.append([out])
        return out

    parent_step(0)
    parent_step(1)
    (square,) = after(chain[-1], square)
    chain.append([square])
    square_rounds = [square, turn(square)]
    parent_step(2)
    block_r = gather_step(0, None)
    late = parent_step(3)
    late_across = lax.ppermute(late, "row", ACROSS)
    late_beside = lax.ppermute(late, "row", SIBLING)
    block_r = gather_step(1, block_r)
    chain.append(chain[-1] + square_rounds[1:])
    block_r = gather_step(2, block_r)
    square_rounds.append(turn(square_rounds[-1]))
    (late_across,) = after(chain[-1], late_across)
    chain.append([late_across])
    late_other = lax.ppermute(late_across, "row", SIBLING)
    wholes[-1] = [late, late_beside, late_across, late_other]
    block_r = gather_step(3, block_r)
    received, kept = [], []
    for n in range(nodes):
        which = (1 - core)[None].astype(jnp.int32)
        sent = transposed(which, taken, n, block_r, chain[-1])
        received.append(lax.ppermute(sent, "row", SIBLING))
        chain.append([sent])
    for n in range(nodes):
        which = core[None].astype(jnp.int32)
        keep = transposed(which, taken, n, block_r, chain[-1])
        kept.append(keep)
        chain.append([keep])
    theirs, mine = halved_sums(here, kept, received, chain[-1] + square_rounds[2:])
    square_rounds.append(turn(square_rounds[-1]))
    chain.append([mine])
    sums = mine + lax.ppermute(theirs, "row", ACROSS)
    terms_one = root_terms(here, zroot, own, sibling, across_same, across_other, chain[-1])
    chain.append([terms_one])
    pairs = pair_terms(heads, block_r, chain[-1])
    chain.append([pairs])
    own_rows, _ = with_parent(choice, square_rounds, whole_j, None, 0, chain[-1])
    blocks_j, terms_two = [], []
    for n in range(nodes):
        own_j = own_rows[:, n * width_two : (n + 1) * width_two]
        blocks_j.append(-(own_j + sums[n]))
        terms_two.append(pairs[n] + jnp.sum(factor_j[n] * own_j, axis=0))
    block_j = jnp.stack(blocks_j)

    share_two = width_two // rows
    packed = jnp.concatenate(
        [terms_one.reshape(rows, share_one)] + [t.reshape(rows, share_two) for t in terms_two],
        axis=1,
    ).reshape(2, 2, -1)
    packed = lax.dynamic_index_in_dim(packed, core, 1, keepdims=False) + lax.ppermute(
        lax.dynamic_index_in_dim(packed, 1 - core, 1, keepdims=False), "row", SIBLING
    )
    packed = lax.dynamic_index_in_dim(packed, chip, 0, keepdims=False) + lax.ppermute(
        lax.dynamic_index_in_dim(packed, 1 - chip, 0, keepdims=False), "row", ACROSS
    )
    var_one = packed[:share_one] + jnp.sum(own_columns * own_columns, axis=0)
    squares = jnp.sum(inv_two * inv_two, axis=1)
    live_share = lax.dynamic_slice_in_dim(live, row * share_two, share_two, 1)
    square_share = lax.dynamic_slice_in_dim(squares, row * share_two, share_two, 1)
    var_two = live_share * (square_share + packed[share_one:].reshape(nodes, share_two))
    return var_one[None, :], var_two, block_j, block_r


def solution(mesh):
    line = mesh.shape["row"] == 4 and mesh.shape["col"] == 4

    def body(*args):
        two_nodes = args[5].shape[0] == 2
        return (line_body if line and two_nodes else general_body)(*args)

    return jax.shard_map(
        body,
        mesh=mesh,
        in_specs=(
            P(("groups", "row"), None),
            P(("groups", "col"), "row", None),
            P(("groups", "col"), None, None),
            P(("groups", "col"), "row", None),
            P(("groups", "col"), "row", None),
            P(("groups", "col"), None, None),
            P(("groups", "col")),
            P(("groups", "col")),
            P(("groups", "col"), "row"),
            P(("groups", "col"), "row"),
        ),
        out_specs=(
            P(("groups", "col"), "row"),
            P(("groups", "col"), "row"),
            P(("groups", "col"), "row", None),
            P(("groups", "col"), "row", None),
        ),
        check_vma=False,
    )
```

```python
import jax
import jax.numpy as jnp
from jax import lax
from jax.experimental import pallas as pl
from jax.experimental.pallas import tpu as pltpu
from jax.sharding import PartitionSpec as P

TILE = 64
CHUNKS = 4


def product(left, right):
    return jnp.dot(left, right, precision=lax.Precision.HIGH, preferred_element_type=jnp.float32)


def product_t(left, right):
    return lax.dot_general(
        left,
        right,
        (((0,), (0,)), ((), ())),
        precision=lax.Precision.HIGH,
        preferred_element_type=jnp.float32,
    )


def batched(form, left, right):
    return jnp.einsum(
        form, left, right, precision=lax.Precision.HIGH, preferred_element_type=jnp.float32
    )


def masked_factors(panel_two_j, panel_two_r, inv_two, live, pattern_j, pattern_r):
    mask_j = jnp.repeat(pattern_j.astype(jnp.float32), TILE, axis=1)
    mask_r = jnp.repeat(pattern_r.astype(jnp.float32), TILE, axis=1)
    masked_j = panel_two_j * mask_j[:, :, None] * live[:, None, :]
    masked_r = panel_two_r * mask_r[:, :, None] * live[:, None, :]
    return batched("nak,nkm->nam", masked_j, inv_two), batched("nak,nkm->nam", masked_r, inv_two)


def live_columns(widths, width_two):
    return (jnp.arange(width_two)[None, :] < widths[:, None]).astype(jnp.float32)


def general_body(
    zroot,
    panel_one,
    inv_one,
    panel_two_j,
    panel_two_r,
    inv_two,
    parents,
    widths,
    pattern_j,
    pattern_r,
):
    rows = lax.axis_size("row")
    row = lax.axis_index("row")
    inverse = inv_one[0]
    width_one = inverse.shape[0]
    share_one = width_one // rows
    nodes, width_two = inv_two.shape[0], inv_two.shape[1]
    factor = product(panel_one[0], inverse)
    own_columns = lax.dynamic_slice_in_dim(inverse, row * share_one, share_one, 1)
    square = product_t(own_columns, inverse)
    factors = lax.all_gather(factor, "col", axis=0)
    squares_of = lax.all_gather(square, "col", axis=0)
    whole = lax.all_gather(factor, "row", axis=0, tiled=True)
    terms = jnp.sum(factor * product(zroot, whole), axis=0)
    var_one = jnp.sum(own_columns * own_columns, axis=0) + lax.psum_scatter(
        terms, "row", scatter_dimension=0, tiled=True
    )
    live = live_columns(widths, width_two)
    factor_j, factor_r = masked_factors(
        panel_two_j, panel_two_r, inv_two, live, pattern_j, pattern_r
    )
    whole_j = lax.all_gather(factor_j, "row", axis=1, tiled=True)
    parent = jnp.take(factors, parents, axis=0)
    parent_square = jnp.take(squares_of, parents, axis=0)
    head = batched("nab,nbm->nam", parent, whole_j) - factor_r
    whole_head = lax.all_gather(head, "row", axis=1, tiled=True)
    block_r = batched("ab,nbm->nam", zroot, whole_head)
    own_j = batched("nab,nbm->nam", parent_square, whole_j)
    block_j = -(
        own_j
        + lax.psum_scatter(
            batched("nab,nam->nbm", parent, block_r), "row", scatter_dimension=1, tiled=True
        )
    )
    terms_two = jnp.sum(head * block_r, axis=1) + jnp.sum(factor_j * own_j, axis=1)
    summed = lax.psum_scatter(terms_two, "row", scatter_dimension=1, tiled=True)
    share_two = summed.shape[1]
    squares = jnp.sum(inv_two * inv_two, axis=1)
    live_share = lax.dynamic_slice_in_dim(live, row * share_two, share_two, 1)
    square_share = lax.dynamic_slice_in_dim(squares, row * share_two, share_two, 1)
    return var_one[None, :], live_share * (square_share + summed), block_j, block_r


ACROSS = [(0, 2), (2, 0), (1, 3), (3, 1)]
SIBLING = [(0, 1), (1, 0), (2, 3), (3, 2)]
DIAGONAL = [(0, 3), (3, 0), (1, 2), (2, 1)]


CHUNKS = 4
VMEM_LIMIT = 48 * 1024 * 1024
ANYWHERE = pl.BlockSpec(memory_space=pl.ANY)
SCALARS = pl.BlockSpec(memory_space=pltpu.SMEM)
WHOLE = pl.BlockSpec(memory_space=pltpu.VMEM)


def cost():
    return pl.CostEstimate(flops=1, bytes_accessed=1, transcendentals=0)


def params(**more):
    return pltpu.CompilerParams(vmem_limit_bytes=VMEM_LIMIT, **more)


def split(x):
    high = x.astype(jnp.bfloat16)
    return high, (x - high.astype(jnp.float32)).astype(jnp.bfloat16)


def three(left, right, contract=((1,), (0,))):
    def dot(a, b):
        return lax.dot_general(a, b, (contract, ((), ())), preferred_element_type=jnp.float32)

    return dot(left[0], right[0]) + (dot(left[0], right[1]) + dot(left[1], right[0]))


def level_one(panel, inverse, sizes):
    root_rows, width = panel.shape
    tile = 256
    starts = [sum(sizes[:q]) for q in range(len(sizes))]

    def kernel(panel_ref, inverse_ref, *refs):
        outs, (high, low) = refs[: len(sizes)], refs[len(sizes) :]

        @pl.when(pl.program_id(0) == 0)
        def _():
            high[...], low[...] = split(panel_ref[...])

        result = three((high[...], low[...]), split(inverse_ref[...]))
        for q, size in enumerate(sizes):
            outs[q][...] = result[starts[q] : starts[q] + size]

    return pl.pallas_call(
        kernel,
        grid=(width // tile,),
        in_specs=[
            pl.BlockSpec((root_rows, width), lambda i: (0, 0)),
            pl.BlockSpec((width, tile), lambda i: (0, i)),
        ],
        out_specs=[pl.BlockSpec((size, tile), lambda i: (0, i)) for size in sizes],
        out_shape=[jax.ShapeDtypeStruct((size, width), jnp.float32) for size in sizes],
        scratch_shapes=[pltpu.VMEM((root_rows, width), jnp.bfloat16)] * 2,
        compiler_params=params(),
        cost_estimate=cost(),
    )(panel, inverse)


def after(deps, *arrays):
    count = len(arrays)

    def kernel(*refs):
        outs = refs[count + len(deps) :]
        for k in range(count):
            outs[k][...] = refs[k][...]

    return pl.pallas_call(
        kernel,
        in_specs=[WHOLE] * count + [ANYWHERE] * len(deps),
        out_specs=[WHOLE] * count,
        out_shape=[jax.ShapeDtypeStruct(x.shape, x.dtype) for x in arrays],
        compiler_params=params(),
        cost_estimate=cost(),
    )(*arrays, *deps)


def square_rows(columns, inverse, deps):
    depth, share = columns.shape
    width = inverse.shape[1]
    tile = 256

    def kernel(columns_ref, inverse_ref, *refs):
        out_ref, high, low = refs[-3:]

        @pl.when(pl.program_id(0) == 0)
        def _():
            high[...], low[...] = split(columns_ref[...])

        out_ref[...] = three((high[...], low[...]), split(inverse_ref[...]), ((0,), (0,)))

    return pl.pallas_call(
        kernel,
        grid=(width // tile,),
        in_specs=[
            pl.BlockSpec((depth, share), lambda i: (0, 0)),
            pl.BlockSpec((depth, tile), lambda i: (0, i)),
        ]
        + [ANYWHERE] * len(deps),
        out_specs=pl.BlockSpec((share, tile), lambda i: (0, i)),
        out_shape=jax.ShapeDtypeStruct((share, width), jnp.float32),
        scratch_shapes=[pltpu.VMEM((depth, share), jnp.bfloat16)] * 2,
        compiler_params=params(),
        cost_estimate=cost(),
    )(columns, inverse, *deps)


def with_parent(choice, rotated, whole_j, minus, start, deps):
    nodes, depth, width = whole_j.shape
    part = rotated[0].shape[0]
    count = len(rotated)
    extra = [] if minus is None else [minus]

    def kernel(choice_ref, *refs):
        whole_ref = refs[count]
        out_ref, chosen_ref, sems = refs[-3:]
        for n in range(nodes):
            for k in range(count):

                @pl.when(choice_ref[n] == k)
                def _():
                    pltpu.make_async_copy(refs[k], chosen_ref.at[n], sems.at[n]).start()

        for n in range(nodes):
            pltpu.make_async_copy(refs[0], chosen_ref.at[n], sems.at[n]).wait()
            result = three(split(chosen_ref[n]), split(whole_ref[n]))
            if extra:
                result = result - refs[count + 1][n, start : start + part, :]
            out_ref[:, n * width : (n + 1) * width] = result

    return pl.pallas_call(
        kernel,
        grid=(1,),
        in_specs=[SCALARS]
        + [ANYWHERE] * count
        + [pl.BlockSpec(x.shape, lambda i: (0, 0, 0)) for x in [whole_j] + extra]
        + [ANYWHERE] * len(deps),
        out_specs=[
            pl.BlockSpec((part, nodes * width), lambda i: (0, 0)),
            pl.BlockSpec((nodes, part, depth), lambda i: (0, 0, 0)),
        ],
        out_shape=[
            jax.ShapeDtypeStruct((part, nodes * width), jnp.float32),
            jax.ShapeDtypeStruct((nodes, part, depth), jnp.float32),
        ],
        scratch_shapes=[pltpu.SemaphoreType.DMA((nodes,))],
        compiler_params=params(),
        cost_estimate=cost(),
    )(choice, *rotated, whole_j, *extra, *deps)


def in_order(order, blocks, deps):
    nodes, share, width = blocks[0].shape
    count = len(blocks)

    def kernel(order_ref, *refs):
        out_ref = refs[-1]
        for k in range(count):
            start = pl.multiple_of(order_ref[k] * share, share)
            for n in range(nodes):
                out_ref[n, pl.ds(start, share), :] = refs[k][n]

    return pl.pallas_call(
        kernel,
        in_specs=[SCALARS] + [WHOLE] * count + [ANYWHERE] * len(deps),
        out_specs=WHOLE,
        out_shape=jax.ShapeDtypeStruct((nodes, count * share, width), jnp.float32),
        compiler_params=params(),
        cost_estimate=cost(),
    )(order, *blocks, *deps)


def halves_of(place, own, deps):
    width = own[0].shape[1]
    half = width // 2
    starts = [sum(x.shape[0] for x in own[:q]) for q in range(len(own))]
    rows = sum(x.shape[0] for x in own)

    def kernel(place_ref, *refs):
        outs = refs[len(own) + len(deps) :]
        for k in range(2):
            at = pl.ds(pl.multiple_of((1 - place_ref[k]) * half, half), half)
            for q, x in enumerate(own):
                outs[k][starts[q] : starts[q] + x.shape[0], :] = refs[q][:, at]

    return pl.pallas_call(
        kernel,
        in_specs=[SCALARS] + [WHOLE] * len(own) + [ANYWHERE] * len(deps),
        out_specs=[WHOLE] * 2,
        out_shape=[jax.ShapeDtypeStruct((rows, half), jnp.float32)] * 2,
        compiler_params=params(),
        cost_estimate=cost(),
    )(place, *own, *deps)


def pair_terms(heads, block_r, deps):
    nodes, _, width = block_r.shape
    starts = [sum(x.shape[0] for x in heads[:q]) for q in range(len(heads))]

    def kernel(*refs):
        block_ref, out_ref = refs[len(heads)], refs[-1]
        for n in range(nodes):
            total = jnp.zeros((1, width), jnp.float32)
            for q, head in enumerate(heads):
                total = total + jnp.sum(
                    refs[q][:, n * width : (n + 1) * width]
                    * block_ref[n, starts[q] : starts[q] + head.shape[0], :],
                    axis=0,
                    keepdims=True,
                )
            out_ref[n : n + 1, :] = total

    return pl.pallas_call(
        kernel,
        in_specs=[WHOLE] * (len(heads) + 1) + [ANYWHERE] * len(deps),
        out_specs=WHOLE,
        out_shape=jax.ShapeDtypeStruct((nodes, width), jnp.float32),
        compiler_params=params(),
        cost_estimate=cost(),
    )(*heads, block_r, *deps)


def root_terms(place, zroot, own, sibling, across_same, across_other, deps):
    root_rows = zroot.shape[0]
    width = own[0].shape[1]
    half = width // 2
    count = len(own)
    starts = [sum(x.shape[0] for x in own[:q]) for q in range(count)]

    def kernel(place_ref, root_ref, *refs):
        sibling_ref, same_ref, other_ref = refs[count : count + 3]
        out_ref, factor = refs[-2:]
        chip, core = place_ref[0], place_ref[1]
        for q, x in enumerate(own):
            factor[starts[q] : starts[q] + x.shape[0], :] = refs[q][...]

        def root(which):
            start = pl.multiple_of(which * root_rows, root_rows)
            return split(root_ref[:, pl.ds(start, root_rows)])

        def halved(which):
            return factor[:, pl.ds(pl.multiple_of(which * half, half), half)]

        def put(which, value):
            at = pl.ds(pl.multiple_of(which * half, half), half)
            out_ref[:, at] = out_ref[:, at] + 2 * jnp.sum(value, axis=0, keepdims=True)

        out_ref[...] = jnp.sum(
            factor[...] * three(root(2 * chip + core), split(factor[...])), axis=0, keepdims=True
        )
        put(core, halved(core) * three(root(2 * chip + 1 - core), split(sibling_ref[...])))
        put(
            chip,
            halved(chip)
            * (
                three(root(2 * (1 - chip) + core), split(same_ref[...]))
                + three(root(2 * (1 - chip) + 1 - core), split(other_ref[...]))
            ),
        )

    return pl.pallas_call(
        kernel,
        in_specs=[SCALARS] + [WHOLE] * (1 + count + 3) + [ANYWHERE] * len(deps),
        out_specs=WHOLE,
        out_shape=jax.ShapeDtypeStruct((1, width), jnp.float32),
        scratch_shapes=[pltpu.VMEM((root_rows, width), jnp.float32)],
        compiler_params=params(),
        cost_estimate=cost(),
    )(place, zroot, *own, sibling, across_same, across_other, *deps)


def root_step(order, zroot, start, parts, before, nodes, deps):
    root_rows = zroot.shape[0]
    size, columns = parts[0].shape
    width = columns // nodes
    count = len(parts)
    tile = 256
    tiles = width // tile
    extra = [] if before is None else [before]

    def kernel(order_ref, root_ref, *refs):
        out_ref, root, high, low, head_high, head_low, sems = refs[-7:]

        @pl.when(pl.program_id(0) == 0)
        def _():
            copies = []
            for k in range(count):
                at = pl.ds(pl.multiple_of(order_ref[k] * root_rows + start, 128), size)
                copies.append(pltpu.make_async_copy(root_ref.at[:, at], root.at[k], sems.at[k]))
                copies[k].start()
            for k in range(count):
                at = slice(k * size, (k + 1) * size)
                copies[k].wait()
                high[:, at], low[:, at] = split(root[k])

        for k in range(count):
            at = slice(k * size, (k + 1) * size)
            head_high[at, :], head_low[at, :] = split(refs[k][...])
        result = three((high[...], low[...]), (head_high[...], head_low[...]))
        out_ref[...] = result + refs[count][...] if extra else result

    block = pl.BlockSpec((None, root_rows, tile), lambda i: (i // tiles, 0, i % tiles))
    return pl.pallas_call(
        kernel,
        grid=(nodes * tiles,),
        in_specs=[SCALARS, ANYWHERE]
        + [pl.BlockSpec((size, tile), lambda i: (0, i))] * count
        + [block] * len(extra)
        + [ANYWHERE] * len(deps),
        out_specs=block,
        out_shape=jax.ShapeDtypeStruct((nodes, root_rows, width), jnp.float32),
        scratch_shapes=[pltpu.VMEM((count, root_rows, size), jnp.float32)]
        + [pltpu.VMEM((root_rows, count * size), jnp.bfloat16)] * 2
        + [pltpu.VMEM((count * size, tile), jnp.bfloat16)] * 2
        + [pltpu.SemaphoreType.DMA((count,))],
        compiler_params=params(),
        cost_estimate=cost(),
    )(order, zroot, *parts, *extra, *deps)


def transposed(which, taken, node, block_r, deps):
    depth = taken[0].shape[2]
    _, rows, width = block_r.shape
    share = depth // 4
    count = len(taken)
    starts = [sum(x.shape[1] for x in taken[:q]) for q in range(count)]

    def kernel(which_ref, *refs):
        block_ref = refs[count]
        out_ref, left = refs[-2:]
        for q, x in enumerate(taken):
            for chip in range(2):
                start = pl.multiple_of((2 * chip + which_ref[0]) * share, share)
                left[
                    starts[q] : starts[q] + x.shape[1], chip * share : (chip + 1) * share
                ] = refs[q][:, pl.ds(start, share)]
        out_ref[...] = three(split(left[...]), split(block_ref[...]), ((0,), (0,)))

    return pl.pallas_call(
        kernel,
        grid=(1,),
        in_specs=[SCALARS]
        + [pl.BlockSpec((None,) + x.shape[1:], lambda i: (node, 0, 0)) for x in taken]
        + [pl.BlockSpec((None, rows, width), lambda i: (node, 0, 0))]
        + [ANYWHERE] * len(deps),
        out_specs=pl.BlockSpec((2 * share, width), lambda i: (0, 0)),
        out_shape=jax.ShapeDtypeStruct((2 * share, width), jnp.float32),
        scratch_shapes=[pltpu.VMEM((rows, 2 * share), jnp.float32)],
        compiler_params=params(),
        cost_estimate=cost(),
    )(which, *taken, block_r, *deps)


def halved_sums(chip, kept, received, deps):
    nodes = len(kept)
    rows, width = kept[0].shape
    share = rows // 2

    def kernel(chip_ref, *refs):
        theirs_ref, mine_ref = refs[-2:]
        for out_ref, which in ((theirs_ref, 1 - chip_ref[0]), (mine_ref, chip_ref[0])):
            at = pl.ds(pl.multiple_of(which * share, share), share)
            for n in range(nodes):
                out_ref[n] = refs[n][at, :] + refs[nodes + n][at, :]

    return pl.pallas_call(
        kernel,
        in_specs=[SCALARS] + [WHOLE] * (2 * nodes) + [ANYWHERE] * len(deps),
        out_specs=[WHOLE] * 2,
        out_shape=[jax.ShapeDtypeStruct((nodes, share, width), jnp.float32)] * 2,
        compiler_params=params(),
        cost_estimate=cost(),
    )(chip, *kept, *received, *deps)


def line_body(
    zroot,
    panel_one,
    inv_one,
    panel_two_j,
    panel_two_r,
    inv_two,
    parents,
    widths,
    pattern_j,
    pattern_r,
):
    rows, cols = 4, 4
    row = lax.axis_index("row")
    col = lax.axis_index("col")
    chip, core = row // 2, row % 2
    root_rows = zroot.shape[0]
    inverse = inv_one[0]
    width_one = inverse.shape[0]
    share_one = width_one // rows
    nodes, width_two = inv_two.shape[0], inv_two.shape[1]

    here = jnp.stack([chip, core]).astype(jnp.int32)

    order = jnp.stack([row, row ^ 1, row ^ 2, row ^ 3]).astype(jnp.int32)
    chain = []

    def exchange(x):
        across = lax.ppermute(x, "row", ACROSS)
        beside = lax.ppermute(x, "row", SIBLING)
        return [x, beside, across, lax.ppermute(across, "row", SIBLING)]

    def turn(x):
        return lax.ppermute(x, "col", [(i, (i + 1) % cols) for i in range(cols)])

    size = root_rows // CHUNKS
    starts = [q * size for q in range(CHUNKS)]
    own = list(level_one(panel_one[0], inverse, [size] * CHUNKS))
    rounds = [own]
    rounds.append([turn(x) for x in own])

    live = live_columns(widths, width_two)
    factor_j, factor_r = masked_factors(
        panel_two_j, panel_two_r, inv_two, live, pattern_j, pattern_r
    )
    (factor_j,) = after([own[0]], factor_j)
    across_j = lax.ppermute(factor_j, "row", ACROSS)
    beside_j = lax.ppermute(factor_j, "row", SIBLING)
    own_columns = lax.dynamic_slice_in_dim(inverse, row * share_one, share_one, 1)
    square = square_rows(own_columns, inverse, [factor_j])
    half = CHUNKS // 2
    (across_j,) = after(rounds[1][:half] + [square, factor_r], across_j)
    other_j = lax.ppermute(across_j, "row", SIBLING)
    to_chip, to_core = halves_of(here, own, [across_j])
    across_same = lax.ppermute(to_chip, "row", ACROSS)
    sibling = lax.ppermute(to_core, "row", SIBLING)
    whole_j = in_order(
        order, [factor_j, beside_j, across_j, other_j], rounds[1][half:] + [to_chip]
    )
    rounds.append([turn(x) for x in rounds[1]])
    (across_same,) = after(rounds[2] + [whole_j, sibling], across_same)
    chain.append([across_same])
    rounds.append([turn(x) for x in rounds[2]])
    across_other = lax.ppermute(across_same, "row", SIBLING)

    heads, taken, wholes = [], [], []
    choice = ((col - parents) % cols).astype(jnp.int32)

    def parent_step(q):
        out, chosen = with_parent(
            choice, [r[q] for r in rounds], whole_j, factor_r, starts[q], chain[-1]
        )
        heads.append(out)
        taken.append(chosen)
        wholes.append(exchange(out) if q < CHUNKS - 1 else None)
        chain.append([out])
        return out

    def gather_step(q, before):
        out = root_step(order, zroot, starts[q], wholes[q], before, nodes, chain[-1])
        chain.append([out])
        return out

    parent_step(0)
    parent_step(1)
    (square,) = after(chain[-1], square)
    chain.append([square])
    square_rounds = [square, turn(square)]
    parent_step(2)
    block_r = gather_step(0, None)
    late = parent_step(3)
    late_across = lax.ppermute(late, "row", ACROSS)
    late_beside = lax.ppermute(late, "row", SIBLING)
    block_r = gather_step(1, block_r)
    chain.append(chain[-1] + square_rounds[1:])
    block_r = gather_step(2, block_r)
    square_rounds.append(turn(square_rounds[-1]))
    (late_across,) = after(chain[-1], late_across)
    chain.append([late_across])
    late_other = lax.ppermute(late_across, "row", SIBLING)
    wholes[-1] = [late, late_beside, late_across, late_other]
    block_r = gather_step(3, block_r)
    received, kept = [], []
    for n in range(nodes):
        which = (1 - core)[None].astype(jnp.int32)
        sent = transposed(which, taken, n, block_r, chain[-1])
        received.append(lax.ppermute(sent, "row", SIBLING))
        chain.append([sent])
    for n in range(nodes):
        which = core[None].astype(jnp.int32)
        keep = transposed(which, taken, n, block_r, chain[-1])
        kept.append(keep)
        chain.append([keep])
    (moved,) = after(chain[-1], square_rounds[-1])
    chain.append([moved])
    square_rounds.append(turn(moved))
    theirs, mine = halved_sums(here, kept, received, chain[-1])
    chain.append([mine])
    sums = mine + lax.ppermute(theirs, "row", ACROSS)
    terms_one = root_terms(here, zroot, own, sibling, across_same, across_other, chain[-1])
    chain.append([terms_one])
    pairs = pair_terms(heads, block_r, chain[-1])
    chain.append([pairs])
    own_rows, _ = with_parent(choice, square_rounds, whole_j, None, 0, chain[-1])
    blocks_j, terms_two = [], []
    for n in range(nodes):
        own_j = own_rows[:, n * width_two : (n + 1) * width_two]
        blocks_j.append(-(own_j + sums[n]))
        terms_two.append(pairs[n] + jnp.sum(factor_j[n] * own_j, axis=0))
    block_j = jnp.stack(blocks_j)

    share_two = width_two // rows
    packed = jnp.concatenate(
        [terms_one.reshape(rows, share_one)] + [t.reshape(rows, share_two) for t in terms_two],
        axis=1,
    )

    def share_of(which):
        return lax.dynamic_index_in_dim(packed, which, 0, keepdims=False)

    packed = (
        share_of(row)
        + lax.ppermute(share_of(row ^ 1), "row", SIBLING)
        + lax.ppermute(share_of(row ^ 2), "row", ACROSS)
        + lax.ppermute(share_of(row ^ 3), "row", DIAGONAL)
    )
    var_one = packed[:share_one] + jnp.sum(own_columns * own_columns, axis=0)
    squares = jnp.sum(inv_two * inv_two, axis=1)
    live_share = lax.dynamic_slice_in_dim(live, row * share_two, share_two, 1)
    square_share = lax.dynamic_slice_in_dim(squares, row * share_two, share_two, 1)
    var_two = live_share * (square_share + packed[share_one:].reshape(nodes, share_two))
    return var_one[None, :], var_two, block_j, block_r


def solution(mesh):
    line = mesh.shape["row"] == 4 and mesh.shape["col"] == 4

    def body(*args):
        two_nodes = args[5].shape[0] == 2
        return (line_body if line and two_nodes else general_body)(*args)

    return jax.shard_map(
        body,
        mesh=mesh,
        in_specs=(
            P(("groups", "row"), None),
            P(("groups", "col"), "row", None),
            P(("groups", "col"), None, None),
            P(("groups", "col"), "row", None),
            P(("groups", "col"), "row", None),
            P(("groups", "col"), None, None),
            P(("groups", "col")),
            P(("groups", "col")),
            P(("groups", "col"), "row"),
            P(("groups", "col"), "row"),
        ),
        out_specs=(
            P(("groups", "col"), "row"),
            P(("groups", "col"), "row"),
            P(("groups", "col"), "row", None),
            P(("groups", "col"), "row", None),
        ),
        check_vma=False,
    )
```

```python
import jax
import jax.numpy as jnp
from jax import lax
from jax.experimental import pallas as pl
from jax.experimental.pallas import tpu as pltpu
from jax.sharding import PartitionSpec as P

TILE = 64
CHUNKS = 4


def product(left, right):
    return jnp.dot(left, right, precision=lax.Precision.HIGH, preferred_element_type=jnp.float32)


def product_t(left, right):
    return lax.dot_general(
        left,
        right,
        (((0,), (0,)), ((), ())),
        precision=lax.Precision.HIGH,
        preferred_element_type=jnp.float32,
    )


def batched(form, left, right):
    return jnp.einsum(
        form, left, right, precision=lax.Precision.HIGH, preferred_element_type=jnp.float32
    )


def masked_factors(panel_two_j, panel_two_r, inv_two, live, pattern_j, pattern_r):
    mask_j = jnp.repeat(pattern_j.astype(jnp.float32), TILE, axis=1)
    mask_r = jnp.repeat(pattern_r.astype(jnp.float32), TILE, axis=1)
    masked_j = panel_two_j * mask_j[:, :, None] * live[:, None, :]
    masked_r = panel_two_r * mask_r[:, :, None] * live[:, None, :]
    return batched("nak,nkm->nam", masked_j, inv_two), batched("nak,nkm->nam", masked_r, inv_two)


def live_columns(widths, width_two):
    return (jnp.arange(width_two)[None, :] < widths[:, None]).astype(jnp.float32)


def general_body(
    zroot,
    panel_one,
    inv_one,
    panel_two_j,
    panel_two_r,
    inv_two,
    parents,
    widths,
    pattern_j,
    pattern_r,
):
    rows = lax.axis_size("row")
    row = lax.axis_index("row")
    inverse = inv_one[0]
    width_one = inverse.shape[0]
    share_one = width_one // rows
    nodes, width_two = inv_two.shape[0], inv_two.shape[1]
    factor = product(panel_one[0], inverse)
    own_columns = lax.dynamic_slice_in_dim(inverse, row * share_one, share_one, 1)
    square = product_t(own_columns, inverse)
    factors = lax.all_gather(factor, "col", axis=0)
    squares_of = lax.all_gather(square, "col", axis=0)
    whole = lax.all_gather(factor, "row", axis=0, tiled=True)
    terms = jnp.sum(factor * product(zroot, whole), axis=0)
    var_one = jnp.sum(own_columns * own_columns, axis=0) + lax.psum_scatter(
        terms, "row", scatter_dimension=0, tiled=True
    )
    live = live_columns(widths, width_two)
    factor_j, factor_r = masked_factors(
        panel_two_j, panel_two_r, inv_two, live, pattern_j, pattern_r
    )
    whole_j = lax.all_gather(factor_j, "row", axis=1, tiled=True)
    parent = jnp.take(factors, parents, axis=0)
    parent_square = jnp.take(squares_of, parents, axis=0)
    head = batched("nab,nbm->nam", parent, whole_j) - factor_r
    whole_head = lax.all_gather(head, "row", axis=1, tiled=True)
    block_r = batched("ab,nbm->nam", zroot, whole_head)
    own_j = batched("nab,nbm->nam", parent_square, whole_j)
    block_j = -(
        own_j
        + lax.psum_scatter(
            batched("nab,nam->nbm", parent, block_r), "row", scatter_dimension=1, tiled=True
        )
    )
    terms_two = jnp.sum(head * block_r, axis=1) + jnp.sum(factor_j * own_j, axis=1)
    summed = lax.psum_scatter(terms_two, "row", scatter_dimension=1, tiled=True)
    share_two = summed.shape[1]
    squares = jnp.sum(inv_two * inv_two, axis=1)
    live_share = lax.dynamic_slice_in_dim(live, row * share_two, share_two, 1)
    square_share = lax.dynamic_slice_in_dim(squares, row * share_two, share_two, 1)
    return var_one[None, :], live_share * (square_share + summed), block_j, block_r


ACROSS = [(0, 2), (2, 0), (1, 3), (3, 1)]
SIBLING = [(0, 1), (1, 0), (2, 3), (3, 2)]
DIAGONAL = [(0, 3), (3, 0), (1, 2), (2, 1)]


CHUNKS = 4
VMEM_LIMIT = 48 * 1024 * 1024
ANYWHERE = pl.BlockSpec(memory_space=pl.ANY)
SCALARS = pl.BlockSpec(memory_space=pltpu.SMEM)
WHOLE = pl.BlockSpec(memory_space=pltpu.VMEM)


def cost():
    return pl.CostEstimate(flops=1, bytes_accessed=1, transcendentals=0)


def params(**more):
    return pltpu.CompilerParams(vmem_limit_bytes=VMEM_LIMIT, **more)


def split(x):
    high = x.astype(jnp.bfloat16)
    return high, (x - high.astype(jnp.float32)).astype(jnp.bfloat16)


def three(left, right, contract=((1,), (0,))):
    def dot(a, b):
        return lax.dot_general(a, b, (contract, ((), ())), preferred_element_type=jnp.float32)

    return dot(left[0], right[0]) + (dot(left[0], right[1]) + dot(left[1], right[0]))


def level_one(panel, inverse, sizes):
    root_rows, width = panel.shape
    tile = 256
    starts = [sum(sizes[:q]) for q in range(len(sizes))]

    def kernel(panel_ref, inverse_ref, *refs):
        outs, (high, low) = refs[: len(sizes)], refs[len(sizes) :]

        @pl.when(pl.program_id(0) == 0)
        def _():
            high[...], low[...] = split(panel_ref[...])

        result = three((high[...], low[...]), split(inverse_ref[...]))
        for q, size in enumerate(sizes):
            outs[q][...] = result[starts[q] : starts[q] + size]

    return pl.pallas_call(
        kernel,
        grid=(width // tile,),
        in_specs=[
            pl.BlockSpec((root_rows, width), lambda i: (0, 0)),
            pl.BlockSpec((width, tile), lambda i: (0, i)),
        ],
        out_specs=[pl.BlockSpec((size, tile), lambda i: (0, i)) for size in sizes],
        out_shape=[jax.ShapeDtypeStruct((size, width), jnp.float32) for size in sizes],
        scratch_shapes=[pltpu.VMEM((root_rows, width), jnp.bfloat16)] * 2,
        compiler_params=params(),
        cost_estimate=cost(),
    )(panel, inverse)


def after(deps, *arrays):
    count = len(arrays)

    def kernel(*refs):
        outs = refs[count + len(deps) :]
        for k in range(count):
            outs[k][...] = refs[k][...]

    return pl.pallas_call(
        kernel,
        in_specs=[WHOLE] * count + [ANYWHERE] * len(deps),
        out_specs=[WHOLE] * count,
        out_shape=[jax.ShapeDtypeStruct(x.shape, x.dtype) for x in arrays],
        compiler_params=params(),
        cost_estimate=cost(),
    )(*arrays, *deps)


def in_place_after(deps, x):
    def kernel(*refs):
        del refs

    return pl.pallas_call(
        kernel,
        in_specs=[ANYWHERE] * (1 + len(deps)),
        out_specs=ANYWHERE,
        out_shape=jax.ShapeDtypeStruct(x.shape, x.dtype),
        input_output_aliases={0: 0},
        compiler_params=params(),
        cost_estimate=cost(),
    )(x, *deps)


def square_rows(columns, inverse, deps):
    depth, share = columns.shape
    width = inverse.shape[1]
    tile = 256

    def kernel(columns_ref, inverse_ref, *refs):
        out_ref, high, low = refs[-3:]

        @pl.when(pl.program_id(0) == 0)
        def _():
            high[...], low[...] = split(columns_ref[...])

        out_ref[...] = three((high[...], low[...]), split(inverse_ref[...]), ((0,), (0,)))

    return pl.pallas_call(
        kernel,
        grid=(width // tile,),
        in_specs=[
            pl.BlockSpec((depth, share), lambda i: (0, 0)),
            pl.BlockSpec((depth, tile), lambda i: (0, i)),
        ]
        + [ANYWHERE] * len(deps),
        out_specs=pl.BlockSpec((share, tile), lambda i: (0, i)),
        out_shape=jax.ShapeDtypeStruct((share, width), jnp.float32),
        scratch_shapes=[pltpu.VMEM((depth, share), jnp.bfloat16)] * 2,
        compiler_params=params(),
        cost_estimate=cost(),
    )(columns, inverse, *deps)


def with_parent(choice, rotated, whole_j, minus, start, deps):
    nodes, depth, width = whole_j.shape
    part = rotated[0].shape[0]
    count = len(rotated)
    extra = [] if minus is None else [minus]

    def kernel(choice_ref, *refs):
        whole_ref = refs[count]
        out_ref, chosen_ref, sems = refs[-3:]
        for n in range(nodes):
            for k in range(count):

                @pl.when(choice_ref[n] == k)
                def _():
                    pltpu.make_async_copy(refs[k], chosen_ref.at[n], sems.at[n]).start()

        for n in range(nodes):
            pltpu.make_async_copy(refs[0], chosen_ref.at[n], sems.at[n]).wait()
            result = three(split(chosen_ref[n]), split(whole_ref[n]))
            if extra:
                result = result - refs[count + 1][n, start : start + part, :]
            out_ref[:, n * width : (n + 1) * width] = result

    return pl.pallas_call(
        kernel,
        grid=(1,),
        in_specs=[SCALARS]
        + [ANYWHERE] * count
        + [pl.BlockSpec(x.shape, lambda i: (0, 0, 0)) for x in [whole_j] + extra]
        + [ANYWHERE] * len(deps),
        out_specs=[
            pl.BlockSpec((part, nodes * width), lambda i: (0, 0)),
            pl.BlockSpec((nodes, part, depth), lambda i: (0, 0, 0)),
        ],
        out_shape=[
            jax.ShapeDtypeStruct((part, nodes * width), jnp.float32),
            jax.ShapeDtypeStruct((nodes, part, depth), jnp.float32),
        ],
        scratch_shapes=[pltpu.SemaphoreType.DMA((nodes,))],
        compiler_params=params(),
        cost_estimate=cost(),
    )(choice, *rotated, whole_j, *extra, *deps)


def in_order(order, blocks, deps):
    nodes, share, width = blocks[0].shape
    count = len(blocks)

    def kernel(order_ref, *refs):
        out_ref = refs[-1]
        for k in range(count):
            start = pl.multiple_of(order_ref[k] * share, share)
            for n in range(nodes):
                out_ref[n, pl.ds(start, share), :] = refs[k][n]

    return pl.pallas_call(
        kernel,
        in_specs=[SCALARS] + [WHOLE] * count + [ANYWHERE] * len(deps),
        out_specs=WHOLE,
        out_shape=jax.ShapeDtypeStruct((nodes, count * share, width), jnp.float32),
        compiler_params=params(),
        cost_estimate=cost(),
    )(order, *blocks, *deps)


def halves_of(place, own, deps):
    width = own[0].shape[1]
    half = width // 2
    starts = [sum(x.shape[0] for x in own[:q]) for q in range(len(own))]
    rows = sum(x.shape[0] for x in own)

    def kernel(place_ref, *refs):
        outs = refs[len(own) + len(deps) :]
        for k in range(2):
            at = pl.ds(pl.multiple_of((1 - place_ref[k]) * half, half), half)
            for q, x in enumerate(own):
                outs[k][starts[q] : starts[q] + x.shape[0], :] = refs[q][:, at]

    return pl.pallas_call(
        kernel,
        in_specs=[SCALARS] + [WHOLE] * len(own) + [ANYWHERE] * len(deps),
        out_specs=[WHOLE] * 2,
        out_shape=[jax.ShapeDtypeStruct((rows, half), jnp.float32)] * 2,
        compiler_params=params(),
        cost_estimate=cost(),
    )(place, *own, *deps)


def pair_terms(heads, block_r, deps):
    nodes, _, width = block_r.shape
    starts = [sum(x.shape[0] for x in heads[:q]) for q in range(len(heads))]

    def kernel(*refs):
        block_ref, out_ref = refs[len(heads)], refs[-1]
        for n in range(nodes):
            total = jnp.zeros((1, width), jnp.float32)
            for q, head in enumerate(heads):
                total = total + jnp.sum(
                    refs[q][:, n * width : (n + 1) * width]
                    * block_ref[n, starts[q] : starts[q] + head.shape[0], :],
                    axis=0,
                    keepdims=True,
                )
            out_ref[n : n + 1, :] = total

    return pl.pallas_call(
        kernel,
        in_specs=[WHOLE] * (len(heads) + 1) + [ANYWHERE] * len(deps),
        out_specs=WHOLE,
        out_shape=jax.ShapeDtypeStruct((nodes, width), jnp.float32),
        compiler_params=params(),
        cost_estimate=cost(),
    )(*heads, block_r, *deps)


def root_terms(place, zroot, own, sibling, across_same, across_other, deps):
    root_rows = zroot.shape[0]
    width = own[0].shape[1]
    half = width // 2
    count = len(own)
    starts = [sum(x.shape[0] for x in own[:q]) for q in range(count)]

    def kernel(place_ref, root_ref, *refs):
        sibling_ref, same_ref, other_ref = refs[count : count + 3]
        out_ref, factor = refs[-2:]
        chip, core = place_ref[0], place_ref[1]
        for q, x in enumerate(own):
            factor[starts[q] : starts[q] + x.shape[0], :] = refs[q][...]

        def root(which):
            start = pl.multiple_of(which * root_rows, root_rows)
            return split(root_ref[:, pl.ds(start, root_rows)])

        def halved(which):
            return factor[:, pl.ds(pl.multiple_of(which * half, half), half)]

        def put(which, value):
            at = pl.ds(pl.multiple_of(which * half, half), half)
            out_ref[:, at] = out_ref[:, at] + 2 * jnp.sum(value, axis=0, keepdims=True)

        out_ref[...] = jnp.sum(
            factor[...] * three(root(2 * chip + core), split(factor[...])), axis=0, keepdims=True
        )
        put(core, halved(core) * three(root(2 * chip + 1 - core), split(sibling_ref[...])))
        put(
            chip,
            halved(chip)
            * (
                three(root(2 * (1 - chip) + core), split(same_ref[...]))
                + three(root(2 * (1 - chip) + 1 - core), split(other_ref[...]))
            ),
        )

    return pl.pallas_call(
        kernel,
        in_specs=[SCALARS] + [WHOLE] * (1 + count + 3) + [ANYWHERE] * len(deps),
        out_specs=WHOLE,
        out_shape=jax.ShapeDtypeStruct((1, width), jnp.float32),
        scratch_shapes=[pltpu.VMEM((root_rows, width), jnp.float32)],
        compiler_params=params(),
        cost_estimate=cost(),
    )(place, zroot, *own, sibling, across_same, across_other, *deps)


def root_step(order, zroot, start, parts, before, nodes, deps):
    root_rows = zroot.shape[0]
    size, columns = parts[0].shape
    width = columns // nodes
    count = len(parts)
    tile = 256
    tiles = width // tile
    extra = [] if before is None else [before]

    def kernel(order_ref, root_ref, *refs):
        out_ref, root, high, low, head_high, head_low, sems = refs[-7:]

        @pl.when(pl.program_id(0) == 0)
        def _():
            copies = []
            for k in range(count):
                at = pl.ds(pl.multiple_of(order_ref[k] * root_rows + start, 128), size)
                copies.append(pltpu.make_async_copy(root_ref.at[:, at], root.at[k], sems.at[k]))
                copies[k].start()
            for k in range(count):
                at = slice(k * size, (k + 1) * size)
                copies[k].wait()
                high[:, at], low[:, at] = split(root[k])

        for k in range(count):
            at = slice(k * size, (k + 1) * size)
            head_high[at, :], head_low[at, :] = split(refs[k][...])
        result = three((high[...], low[...]), (head_high[...], head_low[...]))
        out_ref[...] = result + refs[count][...] if extra else result

    block = pl.BlockSpec((None, root_rows, tile), lambda i: (i // tiles, 0, i % tiles))
    return pl.pallas_call(
        kernel,
        grid=(nodes * tiles,),
        in_specs=[SCALARS, ANYWHERE]
        + [pl.BlockSpec((size, tile), lambda i: (0, i))] * count
        + [block] * len(extra)
        + [ANYWHERE] * len(deps),
        out_specs=block,
        out_shape=jax.ShapeDtypeStruct((nodes, root_rows, width), jnp.float32),
        scratch_shapes=[pltpu.VMEM((count, root_rows, size), jnp.float32)]
        + [pltpu.VMEM((root_rows, count * size), jnp.bfloat16)] * 2
        + [pltpu.VMEM((count * size, tile), jnp.bfloat16)] * 2
        + [pltpu.SemaphoreType.DMA((count,))],
        compiler_params=params(),
        cost_estimate=cost(),
    )(order, zroot, *parts, *extra, *deps)


def transposed(which, taken, node, block_r, deps):
    depth = taken[0].shape[2]
    _, rows, width = block_r.shape
    share = depth // 4
    count = len(taken)
    starts = [sum(x.shape[1] for x in taken[:q]) for q in range(count)]

    def kernel(which_ref, *refs):
        block_ref = refs[count]
        out_ref, left = refs[-2:]
        for q, x in enumerate(taken):
            for chip in range(2):
                start = pl.multiple_of((2 * chip + which_ref[0]) * share, share)
                left[
                    starts[q] : starts[q] + x.shape[1], chip * share : (chip + 1) * share
                ] = refs[q][:, pl.ds(start, share)]
        out_ref[...] = three(split(left[...]), split(block_ref[...]), ((0,), (0,)))

    return pl.pallas_call(
        kernel,
        grid=(1,),
        in_specs=[SCALARS]
        + [pl.BlockSpec((None,) + x.shape[1:], lambda i: (node, 0, 0)) for x in taken]
        + [pl.BlockSpec((None, rows, width), lambda i: (node, 0, 0))]
        + [ANYWHERE] * len(deps),
        out_specs=pl.BlockSpec((2 * share, width), lambda i: (0, 0)),
        out_shape=jax.ShapeDtypeStruct((2 * share, width), jnp.float32),
        scratch_shapes=[pltpu.VMEM((rows, 2 * share), jnp.float32)],
        compiler_params=params(),
        cost_estimate=cost(),
    )(which, *taken, block_r, *deps)


def halved_sums(chip, kept, received, deps):
    nodes = len(kept)
    rows, width = kept[0].shape
    share = rows // 2

    def kernel(chip_ref, *refs):
        theirs_ref, mine_ref = refs[-2:]
        for out_ref, which in ((theirs_ref, 1 - chip_ref[0]), (mine_ref, chip_ref[0])):
            at = pl.ds(pl.multiple_of(which * share, share), share)
            for n in range(nodes):
                out_ref[n] = refs[n][at, :] + refs[nodes + n][at, :]

    return pl.pallas_call(
        kernel,
        in_specs=[SCALARS] + [WHOLE] * (2 * nodes) + [ANYWHERE] * len(deps),
        out_specs=[WHOLE] * 2,
        out_shape=[jax.ShapeDtypeStruct((nodes, share, width), jnp.float32)] * 2,
        compiler_params=params(),
        cost_estimate=cost(),
    )(chip, *kept, *received, *deps)


def line_body(
    zroot,
    panel_one,
    inv_one,
    panel_two_j,
    panel_two_r,
    inv_two,
    parents,
    widths,
    pattern_j,
    pattern_r,
):
    rows, cols = 4, 4
    row = lax.axis_index("row")
    col = lax.axis_index("col")
    chip, core = row // 2, row % 2
    root_rows = zroot.shape[0]
    inverse = inv_one[0]
    width_one = inverse.shape[0]
    share_one = width_one // rows
    nodes, width_two = inv_two.shape[0], inv_two.shape[1]

    here = jnp.stack([chip, core]).astype(jnp.int32)

    order = jnp.stack([row, row ^ 1, row ^ 2, row ^ 3]).astype(jnp.int32)
    chain = []

    def exchange(x):
        across = lax.ppermute(x, "row", ACROSS)
        beside = lax.ppermute(x, "row", SIBLING)
        return [x, beside, across, lax.ppermute(across, "row", SIBLING)]

    def turn(x):
        return lax.ppermute(x, "col", [(i, (i + 1) % cols) for i in range(cols)])

    size = root_rows // CHUNKS
    starts = [q * size for q in range(CHUNKS)]
    own = list(level_one(panel_one[0], inverse, [size] * CHUNKS))
    rounds = [own]
    rounds.append([turn(x) for x in own])

    live = live_columns(widths, width_two)
    factor_j, factor_r = masked_factors(
        panel_two_j, panel_two_r, inv_two, live, pattern_j, pattern_r
    )
    (factor_j,) = after([own[0]], factor_j)
    across_j = lax.ppermute(factor_j, "row", ACROSS)
    beside_j = lax.ppermute(factor_j, "row", SIBLING)
    own_columns = lax.dynamic_slice_in_dim(inverse, row * share_one, share_one, 1)
    square = square_rows(own_columns, inverse, [factor_j])
    half = CHUNKS // 2
    (across_j,) = after(rounds[1][:half] + [square, factor_r], across_j)
    other_j = lax.ppermute(across_j, "row", SIBLING)
    to_chip, to_core = halves_of(here, own, [across_j])
    across_same = lax.ppermute(to_chip, "row", ACROSS)
    sibling = lax.ppermute(to_core, "row", SIBLING)
    whole_j = in_order(
        order, [factor_j, beside_j, across_j, other_j], rounds[1][half:] + [to_chip]
    )
    rounds.append([turn(x) for x in rounds[1]])
    (across_same,) = after(rounds[2] + [whole_j, sibling], across_same)
    chain.append([across_same])
    rounds.append([turn(x) for x in rounds[2]])
    across_other = lax.ppermute(across_same, "row", SIBLING)

    heads, taken, wholes = [], [], []
    choice = ((col - parents) % cols).astype(jnp.int32)

    def parent_step(q):
        out, chosen = with_parent(
            choice, [r[q] for r in rounds], whole_j, factor_r, starts[q], chain[-1]
        )
        heads.append(out)
        taken.append(chosen)
        wholes.append(exchange(out) if q < CHUNKS - 1 else None)
        chain.append([out])
        return out

    def gather_step(q, before):
        out = root_step(order, zroot, starts[q], wholes[q], before, nodes, chain[-1])
        chain.append([out])
        return out

    parent_step(0)
    parent_step(1)
    (square,) = after(chain[-1], square)
    chain.append([square])
    square_rounds = [square, turn(square)]
    parent_step(2)
    block_r = gather_step(0, None)
    late = parent_step(3)
    late_across = lax.ppermute(late, "row", ACROSS)
    late_beside = lax.ppermute(late, "row", SIBLING)
    block_r = gather_step(1, block_r)
    chain.append(chain[-1] + square_rounds[1:])
    block_r = gather_step(2, block_r)
    square_rounds.append(turn(square_rounds[-1]))
    (late_across,) = after(chain[-1], late_across)
    chain.append([late_across])
    late_other = lax.ppermute(late_across, "row", SIBLING)
    wholes[-1] = [late, late_beside, late_across, late_other]
    block_r = gather_step(3, block_r)
    received, kept = [], []
    for n in range(nodes):
        which = (1 - core)[None].astype(jnp.int32)
        sent = transposed(which, taken, n, block_r, chain[-1])
        received.append(lax.ppermute(sent, "row", SIBLING))
        chain.append([sent])
    for n in range(nodes):
        which = core[None].astype(jnp.int32)
        keep = transposed(which, taken, n, block_r, chain[-1])
        kept.append(keep)
        chain.append([keep])
    moved = in_place_after(chain[-1], square_rounds[-1])
    chain.append([moved])
    square_rounds[-1] = moved
    square_rounds.append(turn(moved))
    theirs, mine = halved_sums(here, kept, received, chain[-1])
    chain.append([mine])
    sums = mine + lax.ppermute(theirs, "row", ACROSS)
    terms_one = root_terms(here, zroot, own, sibling, across_same, across_other, chain[-1])
    chain.append([terms_one])
    pairs = pair_terms(heads, block_r, chain[-1])
    chain.append([pairs])
    own_rows, _ = with_parent(choice, square_rounds, whole_j, None, 0, chain[-1])
    blocks_j, terms_two = [], []
    for n in range(nodes):
        own_j = own_rows[:, n * width_two : (n + 1) * width_two]
        blocks_j.append(-(own_j + sums[n]))
        terms_two.append(pairs[n] + jnp.sum(factor_j[n] * own_j, axis=0))
    block_j = jnp.stack(blocks_j)

    share_two = width_two // rows
    packed = jnp.concatenate(
        [terms_one.reshape(rows, share_one)] + [t.reshape(rows, share_two) for t in terms_two],
        axis=1,
    )

    def share_of(which):
        return lax.dynamic_index_in_dim(packed, which, 0, keepdims=False)

    packed = (
        share_of(row)
        + lax.ppermute(share_of(row ^ 1), "row", SIBLING)
        + lax.ppermute(share_of(row ^ 2), "row", ACROSS)
        + lax.ppermute(share_of(row ^ 3), "row", DIAGONAL)
    )
    var_one = packed[:share_one] + jnp.sum(own_columns * own_columns, axis=0)
    squares = jnp.sum(inv_two * inv_two, axis=1)
    live_share = lax.dynamic_slice_in_dim(live, row * share_two, share_two, 1)
    square_share = lax.dynamic_slice_in_dim(squares, row * share_two, share_two, 1)
    var_two = live_share * (square_share + packed[share_one:].reshape(nodes, share_two))
    return var_one[None, :], var_two, block_j, block_r


def solution(mesh):
    line = mesh.shape["row"] == 4 and mesh.shape["col"] == 4

    def body(*args):
        two_nodes = args[5].shape[0] == 2
        return (line_body if line and two_nodes else general_body)(*args)

    return jax.shard_map(
        body,
        mesh=mesh,
        in_specs=(
            P(("groups", "row"), None),
            P(("groups", "col"), "row", None),
            P(("groups", "col"), None, None),
            P(("groups", "col"), "row", None),
            P(("groups", "col"), "row", None),
            P(("groups", "col"), None, None),
            P(("groups", "col")),
            P(("groups", "col")),
            P(("groups", "col"), "row"),
            P(("groups", "col"), "row"),
        ),
        out_specs=(
            P(("groups", "col"), "row"),
            P(("groups", "col"), "row"),
            P(("groups", "col"), "row", None),
            P(("groups", "col"), "row", None),
        ),
        check_vma=False,
    )
```
